32 devices in a mesh: snap: 4 (over x, core), bond: 8 (over z, y).
Axes of the slice: x: 2, y: 2, z: 4, core: 2. Of those that a mesh axis runs over, the one named last changes fastest.
Arguments:
- yields: bfloat16 [4096, 32768], P('snap', 'bond'), may hold values from -60 to 60
- partners: int32 [256, 16], P('bond'), may hold values from -1 to 255, as said below
Outputs:
- bond_means: float32 [32768], P('bond')
- covariance_tiles: float32 [16, 256, 128, 128], P('snap', 'bond')
The draws below stay inside these ranges and needn't reach their ends.
Inputs may be any that keep to these rules, and one draw needn't show every extreme that they name: `partners`: row i lists i first, then distinct blocks in ascending order among i + 1 to i + 56 - 1 (below 256), then -1 in the remaining slots; every row lists at least one block, and some row fills all 16 slots.
All inputs are finite; a program needn't handle non-finite values.
Results may differ from the reference program's by a relative error of at most 0.0007.
Values may be sent and summed in bfloat16 or wider, within the bound.
No kernel may reach another device: no remote copies, remote signals or barrier semaphores. Data moves between devices by JAX's collectives and lax.ppermute only.
A program may use at most 192 MiB of HBM per device.

```python
import math
import jax
import jax.numpy as jnp
from jax import lax

BONDS = 32768
BLOCK = 128
NB = 256
REACH = 56
KMAX = 16
SNAPS = 4096


def draw_yields(key, part):
    keys = jax.random.split(key, 7)
    col_scale = jnp.exp(jax.random.uniform(keys[0], (1, BONDS), jnp.float32, math.log(0.3), math.log(3.0)))
    row_scale = jnp.exp(jax.random.uniform(keys[1], (SNAPS, 1), jnp.float32, math.log(0.5), math.log(2.0)))
    drift = jax.random.uniform(keys[2], (1, BONDS), jnp.float32, -2.0, 2.0)
    factors = jax.random.normal(keys[3], (SNAPS, 8), jnp.float32)
    loadings = jax.random.normal(keys[4], (8, BONDS), jnp.float32) * 0.35
    noise = jax.random.normal(keys[6], (SNAPS, BONDS), jnp.float32)
    common = jnp.dot(factors, loadings, precision=lax.Precision.HIGHEST)
    values = (noise + common) * row_scale * col_scale + drift * col_scale
    return jnp.clip(values, -60.0, 60.0).astype(jnp.bfloat16)


def draw_partners(key, part):
    key_order = jax.random.fold_in(key, 11)
    key_count = jax.random.fold_in(key, 12)
    key_forced = jax.random.fold_in(key, 13)
    block_ids = jnp.arange(NB, dtype=jnp.int32)[:, None]
    offsets = jnp.arange(REACH, dtype=jnp.int32)[None, :]
    scores = jax.random.randint(key_order, (NB, REACH), 0, 1 << 20) * REACH + offsets
    scores = jnp.where(offsets == 0, -1, scores)
    scores = jnp.where(block_ids + offsets >= NB, (1 << 20) * REACH + REACH, scores)
    ordering = jnp.argsort(scores, axis=1)[:, :KMAX].astype(jnp.int32)
    counts = jax.random.randint(key_count, (NB,), 1, KMAX + 1)
    forced = jax.random.randint(key_forced, (), 0, NB - REACH)
    counts = jnp.where(jnp.arange(NB) == forced, KMAX, counts)
    room_left = jnp.minimum(REACH, NB - jnp.arange(NB))
    counts = jnp.minimum(counts, room_left)
    slot_ids = jnp.arange(KMAX)[None, :]
    chosen = jnp.where(slot_ids < counts[:, None], ordering, REACH + 1)
    chosen = jnp.sort(chosen, axis=1)
    return jnp.where(chosen <= REACH - 1, block_ids + chosen, -1).astype(jnp.int32)


def setup_inputs(seed: int = 0) -> dict:
    key_list = jax.random.split(jax.random.key(seed), 3)
    return {
        "yields": draw_yields(jax.random.fold_in(key_list[2], 71), 0),
        "partners": draw_partners(jax.random.fold_in(key_list[2], 71), 0),
    }


def reference(yields, partners):
    column_sums = jnp.sum(yields, axis=0, dtype=jnp.float32)
    bond_means = column_sums / SNAPS
    centered = (yields.astype(jnp.float32) - bond_means[None, :]).astype(jnp.bfloat16)
    blocked = centered.reshape(SNAPS, NB, BLOCK)

    def per_block(args):
        block_row, partner_row = args
        own_block = lax.dynamic_index_in_dim(blocked, block_row, 1, keepdims=False).astype(jnp.float32)
        live_row = partner_row >= 0
        safe_index = jnp.where(live_row, partner_row, 0).astype(jnp.int32)
        chosen = jnp.take(blocked, safe_index, axis=1).astype(jnp.float32)
        tile_sum = jnp.einsum("sa,scb->cab", own_block, chosen, precision=lax.Precision.HIGHEST)
        return tile_sum * live_row.astype(jnp.float32)[:, None, None] / (SNAPS - 1)

    tiles = lax.map(per_block, (jnp.arange(NB, dtype=jnp.int32), partners))
    return bond_means, jnp.transpose(tiles, (1, 0, 2, 3))
```

```python
import functools

import jax
import jax.numpy as jnp
from jax import lax
from jax.experimental import pallas as pl
from jax.experimental.pallas import tpu as pltpu
from jax.sharding import PartitionSpec as P

BLOCK = 128
REACH = 56
CHUNK = 4
WINDOW = 16
UNROLL = 4
CODED = BLOCK + 8
TOP = 10.0
F32 = jnp.float32
BF16 = jnp.bfloat16
ANY = pl.BlockSpec(memory_space=pl.ANY)
SMEM = pl.BlockSpec(memory_space=pltpu.SMEM)
VMEM = pl.BlockSpec(memory_space=pltpu.VMEM)


def params(mib):
    return pltpu.CompilerParams(vmem_limit_bytes=mib << 20)


def from_behind(value, axis, steps):
    count = lax.axis_size(axis)
    first, last = (max(0, -steps), min(count, count - steps))
    return lax.ppermute(value, axis, [(source, source + steps) for source in range(first, last)])


def plain_shards(yields, partners):
    snaps_local, columns = yields.shape
    blocks_local = columns // BLOCK
    total_snaps = snaps_local * lax.axis_size("snap")
    local_sums = jnp.sum(yields, axis=0, dtype=F32)
    totals = lax.psum(local_sums, "snap")
    bond_means = totals / total_snaps
    centered = (yields.astype(F32) - bond_means[None, :]).astype(BF16)
    extent = blocks_local + REACH - 1
    hop_count = (extent - 1) // blocks_local
    pieces = [centered]
    for distance in range(1, hop_count + 1):
        kept_blocks = min(blocks_local, extent - distance * blocks_local)
        kept_cols = kept_blocks * BLOCK
        pieces.append(from_behind(centered[:, :kept_cols], "bond", -distance))
    extended = jnp.concatenate(pieces, axis=1).reshape(snaps_local, -1, BLOCK)
    ext_blocks = extended.shape[1]
    first_block = lax.axis_index("bond") * blocks_local
    live_all = partners >= 0
    index_all = jnp.clip(jnp.where(live_all, partners - first_block, 0), 0, ext_blocks - 1)
    inverse = 1.0 / (total_snaps - 1)

    def block_tiles(args):
        block_row, index_row, live_row = args
        own_block = lax.dynamic_index_in_dim(extended, block_row, 1, keepdims=False)
        chosen = jnp.take(extended, index_row, axis=1)
        tile_sum = jnp.einsum("sa,scb->cab", own_block, chosen, preferred_element_type=F32)
        return tile_sum * (live_row.astype(F32) * inverse)[:, None, None]

    per_block = lax.map(
        block_tiles, (jnp.arange(blocks_local, dtype=jnp.int32), index_all, live_all)
    )
    covariance_tiles = lax.psum_scatter(
        jnp.transpose(per_block, (1, 0, 2, 3)), "snap", scatter_dimension=0, tiled=True
    )
    return (bond_means, covariance_tiles)


def token():
    return jax.ShapeDtypeStruct((8, BLOCK), F32)


def feed_kernel(cfg, plan, info, yields, far, *refs):
    outs = refs[-4 - len(plan):-4]
    buffer, in_sems, out_sems = refs[-3:]
    wide = cfg["chunk"] * BLOCK
    rows = buffer.shape[2]
    odd = info[0]
    pieces = [(n, r) for r in range(buffer.shape[1]) for n in range(len(plan))]

    def fetch(src, cols, n, r):
        part = src.at[pl.ds(r * rows, rows), cols]
        return pltpu.make_async_copy(part, buffer.at[n, r], in_sems.at[n, r])

    def own(n, r):
        return fetch(yields, pl.ds(plan[n][1] * wide, wide), n, r)

    def relayed(n, r):
        return fetch(far, pl.ds(0, wide), n, r)

    def store(n, r):
        part = outs[n].at[pl.ds(r * rows, rows)]
        return pltpu.make_async_copy(buffer.at[n, r], part, out_sems.at[n, r])

    for n, r in pieces:
        kind = plan[n][0]
        if kind == "own":
            own(n, r).start()
        elif kind == "relay":
            relayed(n, r).start()
        else:
            pl.when(odd == 1)(lambda: own(n, r).start())
            pl.when(odd == 0)(lambda: relayed(n, r).start())
    for n, r in pieces:
        relayed(n, r).wait()
        store(n, r).start()
    for n, r in pieces:
        store(n, r).wait()


def feed(cfg, plan, odd, yields, far, *tokens):
    shape = (yields.shape[0], cfg["chunk"] * BLOCK)
    pieces = 4
    return pl.pallas_call(
        functools.partial(feed_kernel, cfg, plan),
        in_specs=[SMEM] + [ANY] * (2 + len(tokens)),
        out_specs=[ANY] * (len(plan) + 1),
        out_shape=[jax.ShapeDtypeStruct(shape, BF16)] * len(plan) + [token()],
        scratch_shapes=[
            pltpu.VMEM((len(plan), pieces, shape[0] // pieces, shape[1]), BF16),
            pltpu.SemaphoreType.DMA((len(plan), pieces)),
            pltpu.SemaphoreType.DMA((len(plan), pieces)),
        ],
        compiler_params=params(16),
        cost_estimate=pl.CostEstimate(flops=0, bytes_accessed=1 << 12, transcendentals=0),
        name="feed",
    )(odd, yields, far, *tokens)


def sums_kernel(raw_ref, _, out_ref):
    out_ref[0] = jnp.sum(raw_ref[...].astype(F32), axis=0, keepdims=True)


def column_sums(yields, after):
    snaps, columns = yields.shape
    wide = 4 * BLOCK
    steps = columns // wide
    return pl.pallas_call(
        sums_kernel,
        grid=(steps,),
        in_specs=[pl.BlockSpec((snaps, wide), lambda i: (0, i)), ANY],
        out_specs=pl.BlockSpec((1, 1, wide), lambda i: (i, 0, 0)),
        out_shape=jax.ShapeDtypeStruct((steps, 1, wide), F32),
        compiler_params=params(16),
        cost_estimate=pl.CostEstimate(flops=0, bytes_accessed=1 << 12, transcendentals=0),
        name="column_sums",
    )(yields, after).reshape(columns)


def transpose_kernel(group, raw_ref, mean_ref, out_ref):
    for g in range(group):
        cols = pl.ds(g * BLOCK, BLOCK)
        block = raw_ref[:, cols].astype(F32) - mean_ref[0, :, cols]
        out_ref[g] = block.T.astype(BF16)


def centered_transposed(yields, means):
    snaps, columns = yields.shape
    group = 2
    blocks = columns // BLOCK
    steps = blocks // group
    return pl.pallas_call(
        functools.partial(transpose_kernel, group),
        grid=(steps,),
        in_specs=[
            pl.BlockSpec((snaps, group * BLOCK), lambda i: (0, i)),
            pl.BlockSpec((1, 1, group * BLOCK), lambda i: (i, 0, 0)),
        ],
        out_specs=pl.BlockSpec((group, BLOCK, snaps), lambda i: (i, 0, 0)),
        out_shape=jax.ShapeDtypeStruct((blocks, BLOCK, snaps), BF16),
        compiler_params=params(24),
        cost_estimate=pl.CostEstimate(flops=0, bytes_accessed=1 << 12, transcendentals=0),
        name="center_transpose",
    )(yields, means.reshape(steps, 1, group * BLOCK))


def tile_loop(lo, hi, load, product, put, store):
    count = hi - lo
    groups = lax.div(count + UNROLL - 1, UNROLL)

    def start_loads(g, half):
        for u in range(UNROLL):
            for copy in load(lo + g * UNROLL + u, half * UNROLL + u):
                copy.start()

    pl.when(groups > 0)(lambda: start_loads(0, 0))

    def body(g, carry):
        half = lax.rem(g, 2)
        base = lo + g * UNROLL
        pl.when(g + 1 < groups)(lambda: start_loads(g + 1, 1 - half))
        for u in range(UNROLL):
            for copy in load(base + u, half * UNROLL + u):
                copy.wait()

        @pl.when(g >= 2)
        def _():
            for u in range(UNROLL):
                store(base + u, half * UNROLL + u).wait()

        values = [product(base + u, half * UNROLL + u) for u in range(UNROLL)]
        for u in range(UNROLL):
            put(half * UNROLL + u, values[u])
        for u in range(UNROLL):
            pl.when(base + u < hi)(lambda: store(base + u, half * UNROLL + u).start())
        return carry

    lax.fori_loop(0, groups, body, 0)

    @pl.when(groups >= 2)
    def _():
        for u in range(UNROLL):
            store(lo, lax.rem(groups, 2) * UNROLL + u).wait()

    @pl.when(groups >= 1)
    def _():
        last = groups - 1
        for u in range(UNROLL):
            pl.when(lo + last * UNROLL + u < hi)(
                lambda: store(lo, lax.rem(last, 2) * UNROLL + u).wait()
            )


def output_place(slots, mlist, out, n):
    v = mlist[n] >> 8
    return out.at[lax.rem(v, slots), lax.div(v, slots)]


def putters(cfg, mlist, out, send, stage, store_sem):
    slots = cfg["slots"]

    def put_out(slot, values):
        stage[slot, 0:BLOCK] = values

    def store_out(n, slot):
        dst = output_place(slots, mlist, out, n)
        return pltpu.make_async_copy(stage.at[slot, pl.ds(0, BLOCK)], dst, store_sem.at[slot])

    def put_send(slot, values):
        top = jnp.maximum(jnp.max(jnp.abs(values), axis=0, keepdims=True), 1e-30)
        power = TOP - jnp.ceil(jnp.log2(top))
        stage[slot, 0:BLOCK] = values * jnp.exp2(power)
        stage[slot, BLOCK:CODED] = jnp.broadcast_to(power, (CODED - BLOCK, BLOCK))

    def store_send(n, slot):
        return pltpu.make_async_copy(stage.at[slot], send.at[n], store_sem.at[slot])

    return put_out, store_out, put_send, store_send


def send_window(info, at, size, send, window, sem):
    copy = pltpu.make_async_copy(send.at[pl.ds(info[at], size)], window, sem)
    copy.start()
    copy.wait()


def own_kernel(
    cfg, info, mlist, olist, xa, xb, _, out, send, window, tok, stage, zero, store_sem, zero_sem,
    win_sem,
):
    slots, inverse = cfg["slots"], cfg["inverse"]
    blocks = xa.shape[0]

    def product(ref):
        def tile(n, slot):
            v = ref[n]
            i = lax.div(v >> 8, slots)
            p = jnp.minimum(v & 255, blocks - 1)
            dims = (((1,), (1,)), ((), ()))
            acc = lax.dot_general(xa[i], xa[p], dims, preferred_element_type=F32)
            acc += lax.dot_general(xb[i], xb[p], dims, preferred_element_type=F32)
            return acc * inverse

        return tile

    def nothing(n, slot):
        return ()

    put_out, store_out, put_send, store_send = putters(cfg, mlist, out, send, stage, store_sem)
    o_lo, m_lo = info[cfg["cut_o"]], info[cfg["cut_m"]]
    o_hi, m_hi = info[cfg["cut_o"] + 1], info[cfg["cut_m"] + 1]
    tile_loop(o_lo, o_hi, nothing, product(olist), put_send, store_send)
    tile_loop(m_lo, m_hi, nothing, product(mlist), put_out, store_out)

    zero[...] = jnp.zeros_like(zero)
    live = info[cfg["cut_m"] + cfg["stages"]]

    def clear(n):
        return pltpu.make_async_copy(zero, output_place(slots, mlist, out, n), zero_sem)

    def start_clear(n, carry):
        clear(n).start()
        return carry

    def wait_clear(n, carry):
        clear(n).wait()
        return carry

    lax.fori_loop(live, slots * blocks, start_clear, 0)
    lax.fori_loop(live, slots * blocks, wait_clear, 0)
    send_window(info, cfg["win_o"], cfg["window"], send, window, win_sem)


def own_stage(cfg, info, mlist, olist, xa, xb, after):
    blocks = xa.shape[0]
    slots, size = cfg["slots"], cfg["window"]
    return pl.pallas_call(
        functools.partial(own_kernel, cfg),
        in_specs=[SMEM, SMEM, SMEM, VMEM, VMEM, ANY],
        out_specs=[ANY] * 4,
        out_shape=[
            jax.ShapeDtypeStruct((slots, blocks, BLOCK, BLOCK), F32),
            jax.ShapeDtypeStruct((slots * blocks + size, CODED, BLOCK), F32),
            jax.ShapeDtypeStruct((size, CODED, BLOCK), F32),
            token(),
        ],
        scratch_shapes=[
            pltpu.VMEM((2 * UNROLL, CODED, BLOCK), F32),
            pltpu.VMEM((BLOCK, BLOCK), F32),
            pltpu.SemaphoreType.DMA((2 * UNROLL,)),
            pltpu.SemaphoreType.DMA,
            pltpu.SemaphoreType.DMA,
        ],
        compiler_params=params(40),
        cost_estimate=pl.CostEstimate(flops=0, bytes_accessed=1 << 16, transcendentals=0),
        name="own_tiles",
    )(info, mlist, olist, xa, xb, after)


def merge_parts(cfg, lo, count, mlist, arrived, out, mine, theirs, mine_sem, theirs_sem):
    slots = cfg["slots"]

    def read_mine(r):
        src = output_place(slots, mlist, out, lo + r)
        return pltpu.make_async_copy(src, mine.at[r], mine_sem.at[r])

    def read_theirs(r):
        return pltpu.make_async_copy(arrived.at[r], theirs.at[r], theirs_sem.at[r])

    def write(r):
        dst = output_place(slots, mlist, out, lo + r)
        return pltpu.make_async_copy(mine.at[r], dst, mine_sem.at[r])

    def first(r, carry):
        read_mine(r).start()
        read_theirs(r).start()
        return carry

    def second(r, carry):
        read_mine(r).wait()
        read_theirs(r).wait()
        scale = jnp.exp2(-theirs[r, BLOCK:BLOCK + 1])
        mine[r] = mine[r] + theirs[r, 0:BLOCK] * scale
        write(r).start()
        return carry

    def third(r, carry):
        write(r).wait()
        return carry

    return tuple(
        lambda step=step: lax.fori_loop(0, count, step, 0) for step in (first, second, third)
    )


def merge_scratch(size):
    return [
        pltpu.VMEM((size, BLOCK, BLOCK), F32),
        pltpu.VMEM((size, CODED, BLOCK), F32),
        pltpu.SemaphoreType.DMA((size,)),
        pltpu.SemaphoreType.DMA((size,)),
    ]


def halo_kernel(cfg, hop, has_far, has_merge, *refs):
    info, mlist, olist, near_mean, far_mean, xa, xb = refs[:7]
    chunk, slots, blocks, inverse = cfg["chunk"], cfg["slots"], cfg["blocks"], cfg["inverse"]
    raw = refs[7:11] if has_far else refs[7:9]
    rest = refs[7 + len(raw):]
    if has_merge:
        arrived, rest = rest[0], rest[1:]
    _, _, _, out, send, window, _ = rest[:7]
    rawbuf, ya, yb, lhs_a, lhs_b, stage, raw_sem, lhs_sem, store_sem, win_sem = rest[7:17]
    step = hop + 1
    o_lo, o_hi = info[cfg["cut_o"] + step], info[cfg["cut_o"] + step + 1]
    m_lo, m_hi = info[cfg["cut_m"] + step], info[cfg["cut_m"] + step + 1]
    near_first = (hop - info[cfg["odd"]]) * chunk
    far_first = hop * chunk
    if has_merge:
        lo = info[cfg["win_m"] + step - 2]
        count = info[cfg["win_m"] + step - 1] - lo
        first, second, third = merge_parts(cfg, lo, count, mlist, arrived, out, *rest[17:])
        first()

    @pl.when(o_hi - o_lo + m_hi - m_lo > 0)
    def _():
        copies = [
            pltpu.make_async_copy(ref, rawbuf.at[n], raw_sem.at[n]) for n, ref in enumerate(raw)
        ]
        for copy in copies:
            copy.start()
        for n, copy in enumerate(copies):
            copy.wait()
            kind, half = n // 2, n % 2
            dst = (ya, yb)[half]
            for j in range(chunk):
                if kind == 0:
                    row = jnp.clip(near_first + j, 0, blocks - 1)
                    mean = near_mean[pl.ds(row, 1), :]
                else:
                    mean = far_mean[pl.ds(far_first + j, 1), :]
                block = rawbuf[n, :, pl.ds(j * BLOCK, BLOCK)].astype(F32) - mean
                dst[kind * chunk + j] = block.astype(BF16)

    def load(ref):
        def copies(n, slot):
            i = lax.div(ref[n] >> 8, slots)
            return (
                pltpu.make_async_copy(xa.at[i], lhs_a.at[slot], lhs_sem.at[slot, 0]),
                pltpu.make_async_copy(xb.at[i], lhs_b.at[slot], lhs_sem.at[slot, 1]),
            )

        return copies

    def product(ref):
        def tile(n, slot):
            rel = ref[n] & 255
            near = rel - blocks - near_first
            far = rel - 2 * blocks - far_first + chunk
            j = jnp.clip(jnp.where(rel >= 2 * blocks, far, near), 0, 2 * chunk - 1)
            acc = jnp.dot(lhs_a[slot], ya[j], preferred_element_type=F32)
            acc += jnp.dot(lhs_b[slot], yb[j], preferred_element_type=F32)
            return acc * inverse

        return tile

    put_out, store_out, put_send, store_send = putters(cfg, mlist, out, send, stage, store_sem)
    tile_loop(o_lo, o_hi, load(olist), product(olist), put_send, store_send)
    tile_loop(m_lo, m_hi, load(mlist), product(mlist), put_out, store_out)
    if has_merge:
        second()
    send_window(info, cfg["win_o"] + step, cfg["window"], send, window, win_sem)
    if has_merge:
        third()


def halo_stage(
    cfg, hop, info, mlist, olist, near_mean, far_mean, xa, xb, raw, arrived, out, send, after
):
    snaps = xa.shape[2]
    chunk, size = cfg["chunk"], cfg["window"]
    has_far, has_merge = len(raw) == 4, arrived is not None
    extra = [arrived] if has_merge else []
    count = 7 + len(raw) + len(extra)
    return pl.pallas_call(
        functools.partial(halo_kernel, cfg, hop, has_far, has_merge),
        in_specs=[SMEM, SMEM, SMEM, VMEM, VMEM] + [ANY] * (count - 2),
        out_specs=[ANY] * 4,
        out_shape=[
            jax.ShapeDtypeStruct(out.shape, F32),
            jax.ShapeDtypeStruct(send.shape, F32),
            jax.ShapeDtypeStruct((size, CODED, BLOCK), F32),
            token(),
        ],
        scratch_shapes=[
            pltpu.VMEM((4, snaps, chunk * BLOCK), BF16),
            pltpu.VMEM((2 * chunk, snaps, BLOCK), BF16),
            pltpu.VMEM((2 * chunk, snaps, BLOCK), BF16),
            pltpu.VMEM((2 * UNROLL, BLOCK, snaps), BF16),
            pltpu.VMEM((2 * UNROLL, BLOCK, snaps), BF16),
            pltpu.VMEM((2 * UNROLL, CODED, BLOCK), F32),
            pltpu.SemaphoreType.DMA((4,)),
            pltpu.SemaphoreType.DMA((2 * UNROLL, 2)),
            pltpu.SemaphoreType.DMA((2 * UNROLL,)),
            pltpu.SemaphoreType.DMA,
        ] + (merge_scratch(size) if has_merge else []),
        input_output_aliases={count: 0, count + 1: 1},
        compiler_params=params(32),
        cost_estimate=pl.CostEstimate(flops=0, bytes_accessed=1 << 16, transcendentals=0),
        name="halo_tiles",
    )(info, mlist, olist, near_mean, far_mean, xa, xb, *raw, *extra, out, send, after)


def merge_kernel(cfg, span, mlist, arrived, _, out, *scratch):
    lo = span[0]
    for part in merge_parts(cfg, lo, span[1] - lo, mlist, arrived, out, *scratch):
        part()


def merge(cfg, span, mlist, arrived, out):
    return pl.pallas_call(
        functools.partial(merge_kernel, cfg),
        in_specs=[SMEM, SMEM, ANY, ANY],
        out_specs=ANY,
        out_shape=jax.ShapeDtypeStruct(out.shape, F32),
        scratch_shapes=merge_scratch(cfg["window"]),
        input_output_aliases={3: 0},
        compiler_params=params(8),
        cost_estimate=pl.CostEstimate(flops=0, bytes_accessed=1 << 14, transcendentals=0),
        name="merge_tiles",
    )(span, mlist, arrived, out)


def work_list(rel, live, stage, stages):
    entries = rel.size
    ids = jnp.arange(entries, dtype=jnp.int32)
    key = jnp.where(live, stage, stages).reshape(-1) * entries + ids
    value = ids * 256 + jnp.where(live, rel, 0).reshape(-1)
    rank = jnp.sum((key[None, :] < key[:, None]).astype(jnp.int32), axis=1)
    ordered = jnp.sum(jnp.where(rank[None, :] == ids[:, None], value[None, :], 0), axis=1)
    bounds = jnp.arange(stages + 1, dtype=jnp.int32) * entries
    cuts = jnp.sum((key[None, :] < bounds[:, None]).astype(jnp.int32), axis=1)
    padded = jnp.pad(ordered.astype(jnp.int32), (0, UNROLL))
    return padded, cuts.astype(jnp.int32)


def window_starts(cuts, stages, size):
    w = jnp.arange(stages + 1, dtype=jnp.int32)
    later = w[:, None] - w[None, :]
    reach = jnp.where(later >= 0, cuts[None, :] + later * size, jnp.int32(1 << 30))
    return jnp.min(reach, axis=1).astype(jnp.int32)


def paired_shards(yields, partners):
    snaps_local, columns = yields.shape
    blocks = columns // BLOCK
    snap_count, bond_count = lax.axis_size("snap"), lax.axis_size("bond")
    total_snaps = snaps_local * snap_count
    q, d = lax.axis_index("snap"), lax.axis_index("bond")
    odd = lax.rem(d, 2).astype(jnp.int32)
    slots = partners.shape[1] // snap_count
    chunk, size = CHUNK, WINDOW
    chunks = blocks // chunk
    far_blocks = REACH - 1 - blocks
    far_chunks = -(-far_blocks // chunk)
    stages = chunks + 2
    cfg = {
        "slots": slots,
        "blocks": blocks,
        "chunk": chunk,
        "window": size,
        "stages": stages,
        "cut_m": 0,
        "cut_o": stages + 1,
        "win_o": 2 * (stages + 1),
        "win_m": 3 * (stages + 1),
        "odd": 4 * (stages + 1),
        "inverse": 1.0 / (total_snaps - 1),
    }

    def other_core(value):
        return lax.ppermute(value, "snap", [(s, s ^ 1) for s in range(snap_count)])

    def other_chip(value):
        halved = value.astype(jnp.float16)
        got = lax.ppermute(halved, "snap", [(s, s ^ 2) for s in range(snap_count)])
        return got.astype(F32)

    down = [(s, s - 2) for s in range(2, bond_count)]
    to_even = [(s, s - 1) for s in range(1, bond_count, 2)]
    to_odd = [(s, s + 1) for s in range(0, bond_count, 2)]
    odd_array = odd[None]

    far, near = [None] * chunks, [None] * (chunks + 1)
    send_far0, send_far1, send_near0, mark = feed(
        cfg, (("own", 0), ("own", 1), ("own", 0)), odd_array, yields, yields
    )
    far[0] = lax.ppermute(send_far0, "bond", down)
    near[0] = lax.ppermute(send_near0, "bond", to_even)
    far[1] = lax.ppermute(send_far1, "bond", down)

    def step(t, *marks):
        last = t + 1 == chunks
        plan = ((("relay" if last else "pick"), t + 1),)
        if t + 2 < chunks:
            plan += (("own", t + 2),)
        made = feed(cfg, plan, odd_array, yields, far[t], *marks)
        near[t + 1] = lax.ppermute(made[0], "bond", to_odd if last else to_even + to_odd)
        if t + 2 < chunks:
            far[t + 2] = lax.ppermute(made[1], "bond", down)
        return made[-1]

    totals = lax.psum(column_sums(yields, mark), "snap")
    bond_means = totals / total_snaps
    near_mean = from_behind(bond_means, "bond", -1).reshape(blocks, BLOCK)
    far_mean = from_behind(bond_means, "bond", -2).reshape(blocks, BLOCK)
    xa = centered_transposed(yields, bond_means)
    xb = other_core(xa)

    rel = partners - d * blocks
    live = partners >= 0
    hop = jnp.where(rel < 2 * blocks, (rel - blocks) // chunk + odd, (rel - 2 * blocks) // chunk)
    stage = jnp.where(rel < blocks, 0, hop + 1)

    def listed(owner):
        def cut(a):
            return lax.dynamic_slice_in_dim(a, owner * slots, slots, axis=1)

        return work_list(cut(rel), cut(live), cut(stage), stages)

    mlist, mcuts = listed(q)
    olist, ocuts = listed(q ^ 2)
    mwin = window_starts(mcuts, stages, size)
    owin = window_starts(ocuts, stages, size)
    left = jnp.maximum(mcuts[-1] - mwin[-1], ocuts[-1] - owin[-1])
    trips = lax.pmax((left + size - 1) // size, ("snap", "bond"))
    info = jnp.concatenate([mcuts, ocuts, owin, mwin, odd_array, trips[None]])

    mark = step(0, mark)
    out, send, window, own_mark = own_stage(cfg, info, mlist, olist, xa, xb, mark)
    arrived = [other_chip(window)]
    mark = step(1, mark, own_mark)
    for t in range(chunks + 1):
        raw = [near[t], other_core(near[t])]
        if t < far_chunks:
            raw += [far[t], other_core(far[t])]
        merged = arrived[t - 1] if t >= 1 else None
        out, send, window, made_mark = halo_stage(
            cfg, t, info, mlist, olist, near_mean, far_mean, xa, xb, raw, merged, out, send, mark
        )
        arrived.append(other_chip(window))
        if t + 2 < chunks:
            mark = step(t + 2, mark, made_mark)
    for w in (stages - 2, stages - 1):
        out = merge(cfg, mwin[w : w + 2], mlist, arrived[w], out)

    def more(state):
        return state[0] < trips

    def turn(state):
        trip, result = state
        at = jnp.minimum(owin[-1] + trip * size, send.shape[0] - size)
        got = other_chip(lax.dynamic_slice_in_dim(send, at, size, axis=0))
        lo = jnp.minimum(mwin[-1] + trip * size, mcuts[-1])
        hi = jnp.minimum(lo + size, mcuts[-1])
        return trip + 1, merge(cfg, jnp.stack([lo, hi]), mlist, got, result)

    _, out = lax.while_loop(more, turn, (jnp.int32(0), out))
    return (bond_means, out)


def shards(yields, partners):
    blocks = yields.shape[1] // BLOCK
    snap_count, bond_count = lax.axis_size("snap"), lax.axis_size("bond")
    two_hops = blocks < REACH - 1 <= 2 * blocks
    if (
        two_hops
        and snap_count == 4
        and bond_count % 2 == 0
        and blocks % CHUNK == 0
        and partners.shape[1] % snap_count == 0
        and yields.shape[0] % BLOCK == 0
    ):
        return paired_shards(yields, partners)
    return plain_shards(yields, partners)


def solution(mesh):
    return jax.shard_map(
        shards,
        mesh=mesh,
        in_specs=(P("snap", "bond"), P("bond", None)),
        out_specs=(P("bond"), P("snap", "bond", None, None)),
        check_vma=False,
    )
```

```python
import functools

import jax
import jax.numpy as jnp
from jax import lax
from jax.experimental import pallas as pl
from jax.experimental.pallas import tpu as pltpu
from jax.sharding import PartitionSpec as P

BLOCK = 128
REACH = 56
CHUNK = 4
WINDOW = 16
PARTS = 8
ROOM = 60
UNROLL = 4
CODED = BLOCK + 8
SEEN = {4: (0,), 6: (1,)}
COSTS = (10000, 10000, 10000, 10000, 500, 10000, 500)
TOP = 10.0
F32 = jnp.float32
BF16 = jnp.bfloat16
ANY = pl.BlockSpec(memory_space=pl.ANY)
SMEM = pl.BlockSpec(memory_space=pltpu.SMEM)
VMEM = pl.BlockSpec(memory_space=pltpu.VMEM)


def params(mib):
    return pltpu.CompilerParams(vmem_limit_bytes=mib << 20)


def from_behind(value, axis, steps):
    count = lax.axis_size(axis)
    first, last = (max(0, -steps), min(count, count - steps))
    return lax.ppermute(value, axis, [(source, source + steps) for source in range(first, last)])


def plain_shards(yields, partners):
    snaps_local, columns = yields.shape
    blocks_local = columns // BLOCK
    total_snaps = snaps_local * lax.axis_size("snap")
    local_sums = jnp.sum(yields, axis=0, dtype=F32)
    totals = lax.psum(local_sums, "snap")
    bond_means = totals / total_snaps
    centered = (yields.astype(F32) - bond_means[None, :]).astype(BF16)
    extent = blocks_local + REACH - 1
    hop_count = (extent - 1) // blocks_local
    pieces = [centered]
    for distance in range(1, hop_count + 1):
        kept_blocks = min(blocks_local, extent - distance * blocks_local)
        kept_cols = kept_blocks * BLOCK
        pieces.append(from_behind(centered[:, :kept_cols], "bond", -distance))
    extended = jnp.concatenate(pieces, axis=1).reshape(snaps_local, -1, BLOCK)
    ext_blocks = extended.shape[1]
    first_block = lax.axis_index("bond") * blocks_local
    live_all = partners >= 0
    index_all = jnp.clip(jnp.where(live_all, partners - first_block, 0), 0, ext_blocks - 1)
    inverse = 1.0 / (total_snaps - 1)

    def block_tiles(args):
        block_row, index_row, live_row = args
        own_block = lax.dynamic_index_in_dim(extended, block_row, 1, keepdims=False)
        chosen = jnp.take(extended, index_row, axis=1)
        tile_sum = jnp.einsum("sa,scb->cab", own_block, chosen, preferred_element_type=F32)
        return tile_sum * (live_row.astype(F32) * inverse)[:, None, None]

    per_block = lax.map(
        block_tiles, (jnp.arange(blocks_local, dtype=jnp.int32), index_all, live_all)
    )
    covariance_tiles = lax.psum_scatter(
        jnp.transpose(per_block, (1, 0, 2, 3)), "snap", scatter_dimension=0, tiled=True
    )
    return (bond_means, covariance_tiles)


def cost(micros):
    return pl.CostEstimate(flops=int(micros * 1e9), bytes_accessed=int(micros * 3e6), transcendentals=0)


def token():
    return jax.ShapeDtypeStruct((8, BLOCK), F32)


def feed_kernel(bounds, plan, odd_ref, yields, far, *refs):
    buffers, (in_sems, out_sems) = refs[-2 - len(plan):-2], refs[-2:]
    outs = refs[-3 - 2 * len(plan):-3 - len(plan)]
    odd = odd_ref[0]
    parts = in_sems.shape[1]
    pieces = [(n, r) for r in range(parts) for n in range(len(plan))]

    def span(ref, r):
        rows = ref.shape[0] // parts
        return pl.ds(r * rows, rows)

    def fetch(src, first, n, r):
        rows, wide = span(src, r), buffers[n].shape[1]
        part = src.at[rows, pl.ds(first * BLOCK, wide)]
        return pltpu.make_async_copy(part, buffers[n].at[rows], in_sems.at[n, r])

    def own(n, r):
        return fetch(yields, bounds[plan[n][1]], n, r)

    def relayed(n, r):
        return fetch(far, 0, n, r)

    def store(n, r):
        rows = span(yields, r)
        return pltpu.make_async_copy(buffers[n].at[rows], outs[n].at[rows], out_sems.at[n, r])

    for n, r in pieces:
        if plan[n][0] == "own":
            own(n, r).start()
        else:
            pl.when(odd == 1)(lambda: own(n, r).start())
            pl.when(odd == 0)(lambda: relayed(n, r).start())
    for n, r in pieces:
        own(n, r).wait()
        store(n, r).start()
    for n, r in pieces:
        store(n, r).wait()


def feed(cfg, plan, odd, yields, far, *tokens):
    bounds, parts = cfg["bounds"], 4
    shapes = [(yields.shape[0], (bounds[t + 1] - bounds[t]) * BLOCK) for _, t in plan]
    return pl.pallas_call(
        functools.partial(feed_kernel, bounds, plan),
        in_specs=[SMEM] + [ANY] * (2 + len(tokens)),
        out_specs=[ANY] * (len(plan) + 1),
        out_shape=[jax.ShapeDtypeStruct(shape, BF16) for shape in shapes] + [token()],
        scratch_shapes=[pltpu.VMEM(shape, BF16) for shape in shapes]
        + [pltpu.SemaphoreType.DMA((len(plan), parts))] * 2,
        compiler_params=params(ROOM),
        cost_estimate=cost(COSTS[0]),
        name="feed",
    )(odd, yields, far, *tokens)


def rest_kernel(_, out):
    pass


def rest(after):
    return pl.pallas_call(
        rest_kernel,
        in_specs=[ANY],
        out_specs=ANY,
        out_shape=token(),
        compiler_params=params(ROOM),
        cost_estimate=cost(COSTS[0]),
        name="rest",
    )(after)


def sums_kernel(raw_ref, _, out_ref):
    out_ref[0] = jnp.sum(raw_ref[...].astype(F32), axis=0, keepdims=True)


def column_sums(yields, after):
    snaps, columns = yields.shape
    wide = 4 * BLOCK
    steps = columns // wide
    return pl.pallas_call(
        sums_kernel,
        grid=(steps,),
        in_specs=[pl.BlockSpec((snaps, wide), lambda i: (0, i)), ANY],
        out_specs=pl.BlockSpec((1, 1, wide), lambda i: (i, 0, 0)),
        out_shape=jax.ShapeDtypeStruct((steps, 1, wide), F32),
        compiler_params=params(ROOM),
        cost_estimate=cost(COSTS[1]),
        name="column_sums",
    )(yields, after).reshape(columns)


def transpose_kernel(group, raw_ref, mean_ref, out_ref):
    for g in range(group):
        cols = pl.ds(g * BLOCK, BLOCK)
        block = raw_ref[:, cols].astype(F32) - mean_ref[0, :, cols]
        out_ref[g] = block.T.astype(BF16)


def centered_transposed(yields, means):
    snaps, columns = yields.shape
    group = 2
    blocks = columns // BLOCK
    steps = blocks // group
    return pl.pallas_call(
        functools.partial(transpose_kernel, group),
        grid=(steps,),
        in_specs=[
            pl.BlockSpec((snaps, group * BLOCK), lambda i: (0, i)),
            pl.BlockSpec((1, 1, group * BLOCK), lambda i: (i, 0, 0)),
        ],
        out_specs=pl.BlockSpec((group, BLOCK, snaps), lambda i: (i, 0, 0)),
        out_shape=jax.ShapeDtypeStruct((blocks, BLOCK, snaps), BF16),
        compiler_params=params(ROOM),
        cost_estimate=cost(COSTS[2]),
        name="center_transpose",
    )(yields, means.reshape(steps, 1, group * BLOCK))


def entry(entries, n):
    v = entries[n]
    return (v >> 12) & 63, (v >> 8) & 15, v & 255


def travels(entries, n):
    return (entries[n] >> 18) & 1 == 1


def output_place(entries, out, n):
    row, slot, _ = entry(entries, n)
    return out.at[slot, row]


def all_rows(xa, xb, rows_a, rows_b, sems):
    rows = xa.shape[0] // PARTS

    def copies(part):
        span = pl.ds(part * rows, rows)
        return (
            pltpu.make_async_copy(xa.at[span], rows_a.at[span], sems.at[0, part]),
            pltpu.make_async_copy(xb.at[span], rows_b.at[span], sems.at[1, part]),
        )

    def start():
        for part in reversed(range(PARTS)):
            for copy in copies(part):
                copy.start()

    def wait_down_to(here, need):
        for part in reversed(range(PARTS)):

            @pl.when((here > part) & (need <= part))
            def _():
                for copy in copies(part):
                    copy.wait()

        return jnp.minimum(here, need)

    def begin(g, wanted):
        pass

    def ready(g, here, wanted):
        lowest = functools.reduce(jnp.minimum, wanted)
        need = sum(((lowest >= part * rows).astype(jnp.int32) for part in range(1, PARTS)), 0)
        return wait_down_to(here, need)

    def finish(here):
        wait_down_to(here, 0)

    return start, (begin, ready, finish)


def few_rows(xa, xb, rows_a, rows_b, sems):
    def copies(g, wanted):
        for u, row in enumerate(wanted):
            at = (g & 1) * UNROLL + u
            yield pltpu.make_async_copy(xa.at[row], rows_a.at[at], sems.at[0, at])
            yield pltpu.make_async_copy(xb.at[row], rows_b.at[at], sems.at[1, at])

    def begin(g, wanted):
        for copy in copies(g, wanted):
            copy.start()

    def ready(g, here, wanted):
        for copy in copies(g, wanted):
            copy.wait()
        return here

    def finish(here):
        pass

    return begin, ready, finish


def tile_loop(cfg, step, info, work, out, send, stage, store_sem, rows_in, product):
    lo = info[cfg["cut_o"] + step] + info[cfg["cut_m"] + step]
    hi = info[cfg["cut_o"] + step + 1] + info[cfg["cut_m"] + step + 1]
    groups = lax.div(hi - lo + UNROLL - 1, UNROLL)
    begin, ready, finish = rows_in

    def rows_of(g):
        return [entry(work, lo + g * UNROLL + u)[0] for u in range(UNROLL)]

    def each_store(g, act):
        for u in range(UNROLL):
            n, at = lo + g * UNROLL + u, (g & 1) * UNROLL + u
            away = travels(work, n)

            @pl.when((n < hi) & away)
            def _():
                dst = send.at[work[n] >> 19]
                act(pltpu.make_async_copy(stage.at[at], dst, store_sem.at[at]))

            @pl.when((n < hi) & jnp.logical_not(away))
            def _():
                src, dst = stage.at[at, pl.ds(0, BLOCK)], output_place(work, out, n)
                act(pltpu.make_async_copy(src, dst, store_sem.at[at]))

    pl.when(groups > 0)(lambda: begin(0, rows_of(0)))

    def body(g, here):
        base = lo + g * UNROLL
        found = [entry(work, base + u) for u in range(UNROLL)]
        pl.when(g + 1 < groups)(lambda: begin(g + 1, rows_of(g + 1)))
        here = ready(g, here, [row for row, _, _ in found])
        pl.when(g >= 2)(lambda: each_store(g - 2, lambda copy: copy.wait()))
        values = [
            product((g & 1) * UNROLL + u, row, rel) for u, (row, _, rel) in enumerate(found)
        ]
        for u in range(UNROLL):
            at = (g & 1) * UNROLL + u
            top = jnp.maximum(jnp.max(jnp.abs(values[u]), axis=0, keepdims=True), 1e-30)
            power = jnp.where(travels(work, base + u), TOP - jnp.ceil(jnp.log2(top)), 0.0)
            stage[at, 0:BLOCK] = values[u] * jnp.exp2(power)
            stage[at, BLOCK:CODED] = jnp.broadcast_to(power, (CODED - BLOCK, BLOCK))
        each_store(g, lambda copy: copy.start())
        return here

    finish(lax.fori_loop(0, groups, body, jnp.int32(PARTS)))
    pl.when(groups >= 2)(lambda: each_store(groups - 2, lambda copy: copy.wait()))
    pl.when(groups >= 1)(lambda: each_store(groups - 1, lambda copy: copy.wait()))


def send_window(info, at, send, window, sem):
    copy = pltpu.make_async_copy(send.at[pl.ds(info[at], window.shape[0])], window, sem)
    copy.start()
    copy.wait()


def stage_scratch(xa, rows):
    return [
        pltpu.VMEM((rows,) + xa.shape[1:], BF16),
        pltpu.VMEM((rows,) + xa.shape[1:], BF16),
        pltpu.VMEM((2 * UNROLL, CODED, BLOCK), F32),
        pltpu.SemaphoreType.DMA((2, max(PARTS, 2 * UNROLL))),
        pltpu.SemaphoreType.DMA((2 * UNROLL,)),
        pltpu.SemaphoreType.DMA,
    ]


def own_kernel(cfg, info, mlist, work, means, xa, xb, *refs):
    means_out, refs = refs[-13], refs[-12:]
    means_out[...] = means[...]
    out, send, window, _, rows_a, rows_b, stage, row_sem, store_sem, sem, zero, zero_sem = refs
    start_rows, rows_in = all_rows(xa, xb, rows_a, rows_b, row_sem)
    start_rows()

    def product(at, row, rel):
        p = jnp.minimum(rel, xa.shape[0] - 1)
        dims = (((1,), (1,)), ((), ()))
        acc = lax.dot_general(rows_a[row], rows_a[p], dims, preferred_element_type=F32)
        acc += lax.dot_general(rows_b[row], rows_b[p], dims, preferred_element_type=F32)
        return acc * cfg["inverse"]

    zero[...] = jnp.zeros_like(zero)

    def clear(n):
        return pltpu.make_async_copy(zero, output_place(mlist, out, n), zero_sem)

    def start_clear(n, carry):
        clear(n).start()
        return carry

    def wait_clear(n, carry):
        clear(n).wait()
        return carry

    live = info[cfg["cut_m"] + cfg["stages"]]
    tile_loop(cfg, 0, info, work, out, send, stage, store_sem, rows_in, product)
    lax.fori_loop(live, cfg["entries"], start_clear, 0)
    send_window(info, cfg["win_o"], send, window, sem)
    lax.fori_loop(live, cfg["entries"], wait_clear, 0)


def own_stage(cfg, info, mlist, work, means, xa, xb, *after):
    blocks = xa.shape[0]
    room = max(cfg["windows"] + (WINDOW,))
    return pl.pallas_call(
        functools.partial(own_kernel, cfg),
        in_specs=[SMEM] * 3 + [VMEM] + [ANY] * (2 + len(after)),
        out_specs=[VMEM, ANY, ANY, VMEM, ANY],
        out_shape=[
            jax.ShapeDtypeStruct(means.shape, F32),
            jax.ShapeDtypeStruct((cfg["slots"], blocks, BLOCK, BLOCK), F32),
            jax.ShapeDtypeStruct((cfg["entries"] + room, CODED, BLOCK), F32),
            jax.ShapeDtypeStruct((cfg["windows"][0], CODED, BLOCK), F32),
            token(),
        ],
        scratch_shapes=stage_scratch(xa, blocks)
        + [pltpu.VMEM((BLOCK, BLOCK), F32), pltpu.SemaphoreType.DMA],
        compiler_params=params(ROOM),
        cost_estimate=cost(COSTS[3]),
        name="own_tiles",
    )(info, mlist, work, means, xa, xb, *after)


def merge_parts(cfg, lo, count, mlist, arrived, out, mine, theirs, mine_sem, theirs_sem):
    def read_mine(r):
        src = output_place(mlist, out, lo + r)
        return pltpu.make_async_copy(src, mine.at[r], mine_sem.at[r])

    def read_theirs(r):
        return pltpu.make_async_copy(arrived.at[r], theirs.at[r], theirs_sem.at[r])

    def write(r):
        dst = output_place(mlist, out, lo + r)
        return pltpu.make_async_copy(mine.at[r], dst, mine_sem.at[r])

    def first(r, carry):
        read_mine(r).start()
        read_theirs(r).start()
        return carry

    def second(r, carry):
        read_mine(r).wait()
        read_theirs(r).wait()
        scale = jnp.exp2(-theirs[r, BLOCK:BLOCK + 1])
        mine[r] = mine[r] + theirs[r, 0:BLOCK] * scale
        write(r).start()
        return carry

    def third(r, carry):
        write(r).wait()
        return carry

    return tuple(
        lambda step=step: lax.fori_loop(0, count, step, 0) for step in (first, second, third)
    )


def merge_scratch(size):
    return [
        pltpu.VMEM((size, BLOCK, BLOCK), F32),
        pltpu.VMEM((size, CODED, BLOCK), F32),
        pltpu.SemaphoreType.DMA((size,)),
        pltpu.SemaphoreType.DMA((size,)),
    ]


def join_kernel(spans, *refs):
    kinds = 2 if len(spans) > 0 and any(kind for kind, _, _ in spans) else 1
    means, refs = refs[:kinds], refs[kinds:]
    raw = refs[:len(spans)]
    out, _, rawbuf, done, raw_sem, out_sem = refs[-6:]
    places = [(n, kind, first, j) for n, (kind, first, w) in enumerate(spans) for j in range(w)]

    def fetch(at):
        n, _, _, j = places[at]
        src = raw[n].at[:, pl.ds(j * BLOCK, BLOCK)]
        return pltpu.make_async_copy(src, rawbuf.at[at], raw_sem.at[at])

    def store(at):
        return pltpu.make_async_copy(done.at[at], out.at[at], out_sem.at[at])

    for at in range(len(places)):
        fetch(at).start()
    for at, (_, kind, first, j) in enumerate(places):
        fetch(at).wait()
        block = rawbuf[at].astype(F32) - means[kind][first + j:first + j + 1, :]
        done[at] = block.astype(BF16)
        store(at).start()
    for at in range(len(places)):
        store(at).wait()


def join(means, raw, spans, *after):
    snaps = raw[0].shape[0]
    kinds = 2 if any(kind for kind, _, _ in spans) else 1
    blocks = (sum(w for _, _, w in spans), snaps, BLOCK)
    return pl.pallas_call(
        functools.partial(join_kernel, spans),
        in_specs=[VMEM] * kinds + [ANY] * (len(raw) + len(after)),
        out_specs=[ANY, ANY],
        out_shape=[jax.ShapeDtypeStruct(blocks, BF16), token()],
        scratch_shapes=[
            pltpu.VMEM(blocks, BF16),
            pltpu.VMEM(blocks, BF16),
            pltpu.SemaphoreType.DMA((blocks[0],)),
            pltpu.SemaphoreType.DMA((blocks[0],)),
        ],
        compiler_params=params(ROOM),
        cost_estimate=cost(COSTS[4]),
        name="center_join",
    )(*means[:kinds], *raw, *after)


def halo_kernel(cfg, step, merges, *refs):
    info, mlist, work, cast, xa, xb = refs[:6]
    ca, cb = refs[6:8]
    refs = refs[8:]
    blocks = cfg["blocks"]
    first_block, end_block = cfg["spans"][step - 1]
    arrived, rest = refs[:len(merges)], refs[len(merges):]
    out, send, _, vote = rest[3:7]
    rest = rest[7:]
    if cfg["windows"][step]:
        window, rest = rest[0], rest[1:]
    rows_a, rows_b, stage, row_sem, store_sem, sem, ya, yb, raw_sem = rest[:9]
    vote[0] = cast[0]
    rows_in = few_rows(xa, xb, rows_a, rows_b, row_sem)
    halves = [
        pltpu.make_async_copy(src, dst, raw_sem.at[n])
        for n, (src, dst) in enumerate(((ca, ya), (cb, yb)))
    ]
    for copy in halves:
        copy.start()
    parts = []
    for n, w in enumerate(merges):
        lo = info[cfg["win_m"] + w]
        count = info[cfg["win_m"] + w + 1] - lo
        parts.append(merge_parts(cfg, lo, count, mlist, arrived[n], out, *rest[9 + 4 * n:13 + 4 * n]))
    for first, _, _ in parts:
        first()
    for copy in halves:
        copy.wait()

    def product(at, row, rel):
        near = rel - blocks - first_block
        far = rel - 2 * blocks - first_block + end_block - first_block
        j = jnp.clip(jnp.where(rel >= 2 * blocks, far, near), 0, ya.shape[0] - 1)
        acc = jnp.dot(rows_a[at], ya[j], preferred_element_type=F32)
        acc += jnp.dot(rows_b[at], yb[j], preferred_element_type=F32)
        return acc * cfg["inverse"]

    tile_loop(cfg, step, info, work, out, send, stage, store_sem, rows_in, product)
    for _, second, _ in parts:
        second()
    if cfg["windows"][step]:
        send_window(info, cfg["win_o"] + step, send, window, sem)
    for _, _, third in parts:
        third()


def halo_stage(cfg, step, merges, info, mlist, work, cast, xa, xb, halves, arrived, out, send, after):
    count = 6 + len(halves) + len(arrived)
    size = cfg["windows"][step]
    shapes = [
        jax.ShapeDtypeStruct(out.shape, F32),
        jax.ShapeDtypeStruct(send.shape, F32),
        token(),
        jax.ShapeDtypeStruct((1,), jnp.int32),
        jax.ShapeDtypeStruct((size, CODED, BLOCK), F32),
    ]
    scratch = stage_scratch(xa, 2 * UNROLL) + [
        pltpu.VMEM(halves[0].shape[-3:], BF16),
        pltpu.VMEM(halves[0].shape[-3:], BF16),
        pltpu.SemaphoreType.DMA((2,)),
    ]
    for window in arrived:
        scratch += merge_scratch(window.shape[0])
    made = pl.pallas_call(
        functools.partial(halo_kernel, cfg, step, merges),
        in_specs=[SMEM] * 4 + [ANY] * (count - 1),
        out_specs=[ANY, ANY, ANY, SMEM, VMEM][:5 if size else 4],
        out_shape=shapes[:5 if size else 4],
        scratch_shapes=scratch,
        input_output_aliases={count: 0, count + 1: 1},
        compiler_params=params(ROOM),
        cost_estimate=cost(COSTS[5]),
        name="halo_tiles",
    )(info, mlist, work, cast, xa, xb, *halves, *arrived, out, send, after)
    return made if size else (*made, None)


def merge_kernel(cfg, span, mlist, arrived, _, out, *scratch):
    lo = span[0]
    for part in merge_parts(cfg, lo, span[1] - lo, mlist, arrived, out, *scratch):
        part()


def merge(cfg, span, mlist, arrived, out):
    return pl.pallas_call(
        functools.partial(merge_kernel, cfg),
        in_specs=[SMEM, SMEM, ANY, ANY],
        out_specs=ANY,
        out_shape=jax.ShapeDtypeStruct(out.shape, F32),
        scratch_shapes=merge_scratch(arrived.shape[0]),
        input_output_aliases={3: 0},
        compiler_params=params(ROOM),
        cost_estimate=cost(COSTS[6]),
        name="merge_tiles",
    )(span, mlist, arrived, out)


def work_list(value, stage):
    entries = value.size
    ids = jnp.arange(entries, dtype=jnp.int32)
    key = (stage + 1) * entries - ids
    rank = jnp.sum((key[None, :] < key[:, None]).astype(jnp.int32), axis=1).astype(jnp.int32)
    ordered = jnp.sum(jnp.where(rank[None, :] == ids[:, None], value[None, :], 0), axis=1)
    return jnp.pad(ordered.astype(jnp.int32), (0, UNROLL)), rank


def window_starts(cuts, sizes):
    sent = jnp.array([sum(sizes[:w]) for w in range(len(sizes) + 1)], jnp.int32)
    later = sent[:, None] - sent[None, :]
    reach = jnp.where(later >= 0, cuts[..., None, :] + later, jnp.int32(1 << 30))
    return jnp.min(reach, axis=-1).astype(jnp.int32)


def hop_plan(blocks):
    hops = blocks // CHUNK
    stages = [(t, t + 1) for t in range(0, hops - 2, 2)] + [(hops - 2,), (hops - 1,)]
    return tuple(range(0, blocks + 1, CHUNK)), tuple(stages)


def paired_shards(yields, partners):
    snaps_local, columns = yields.shape
    blocks = columns // BLOCK
    snap_count, bond_count = lax.axis_size("snap"), lax.axis_size("bond")
    total_snaps = snaps_local * snap_count
    q, d = lax.axis_index("snap"), lax.axis_index("bond")
    odd = lax.rem(d, 2).astype(jnp.int32)[None]
    slots = partners.shape[1] // snap_count
    bounds, takes = hop_plan(blocks)
    hops = len(bounds) - 1
    far_blocks = REACH - 1 - blocks
    stages = len(takes) + 1
    windows = (3 * WINDOW,) + (2 * WINDOW,) * (stages - 4) + (0, WINDOW + 8, WINDOW + 4)
    cfg = {
        "entries": blocks * slots,
        "spans": tuple((bounds[hop[0]], bounds[hop[-1] + 1]) for hop in takes),
        "slots": slots,
        "blocks": blocks,
        "bounds": bounds,
        "windows": windows,
        "stages": stages,
        "cut_m": 0,
        "cut_o": stages + 1,
        "win_o": 2 * (stages + 1),
        "win_m": 3 * (stages + 1),
        "inverse": 1.0 / (total_snaps - 1),
    }

    def other_core(value):
        return lax.ppermute(value, "snap", [(s, s ^ 1) for s in range(snap_count)])

    def across(value):
        return lax.ppermute(value, "snap", [(s, s ^ 2) for s in range(snap_count)])

    def other_chip(value):
        return across(value.astype(jnp.float16)).astype(F32)

    far, near = [None] * hops, [None] * hops

    def send_far(t, value):
        far[t] = lax.ppermute(value, "bond", [(s, s - 2) for s in range(2, bond_count)])

    def send_near(t, value):
        near[t] = lax.ppermute(value, "bond", [(s, s ^ 1) for s in range(bond_count)])

    second, mark = feed(cfg, (("own", 1),), odd, yields, yields)
    send_far(1, second)
    first, mark = feed(cfg, (("own", 0),), odd, yields, yields, mark)
    send_far(0, first)

    def step(t, *marks):
        plan = (("pick", t),)
        if t < hops - 2:
            plan += (("own", t + 2),)
        made = feed(cfg, plan, odd, yields, far[t], *marks)
        send_near(t, made[0])
        if len(plan) == 2:
            send_far(t + 2, made[1])
        return made[-1]

    sums = column_sums(yields, mark)
    sums = sums + other_core(sums)
    totals = sums + across(sums)
    bond_means = totals / total_snaps
    xa = centered_transposed(yields, bond_means)
    xb = other_core(xa)

    rel = partners - d * blocks
    live = partners >= 0
    halo_block = jnp.where(rel < 2 * blocks, rel - blocks, rel - 2 * blocks)
    ends = jnp.array([end for _, end in cfg["spans"][:-1]], jnp.int32)
    taken = jnp.sum((halo_block[..., None] >= ends).astype(jnp.int32), axis=-1)
    stage = jnp.where(live, jnp.where(rel < blocks, 0, taken + 1), stages)
    groups = stage.reshape(blocks, snap_count, slots)
    marks = jnp.arange(stages + 1, dtype=jnp.int32)
    cuts = jnp.sum((groups[..., None] < marks).astype(jnp.int32), axis=(0, 2))
    starts = window_starts(cuts, windows)
    left = jnp.max(cuts[:, -1] - starts[:, -1])

    def row_of(table, owner):
        return lax.dynamic_index_in_dim(table, owner, 0, keepdims=False)

    def listed(owner):
        def cut(a):
            return lax.dynamic_slice_in_dim(a, owner * slots, slots, axis=1)

        rows = lax.broadcasted_iota(jnp.int32, (blocks, slots), 0)
        value = rows * 4096 + lax.broadcasted_iota(jnp.int32, (blocks, slots), 1) * 256
        value, when = value + cut(jnp.where(live, rel, 0)), cut(stage)
        ordered, rank = work_list(value.reshape(-1), when.reshape(-1))
        return value, when, ordered, rank.reshape(blocks, slots)

    mvalue, mstage, mlist, _ = listed(q)
    ovalue, ostage, _, orank = listed(q ^ 2)
    ovalue = ovalue + (2 * orank + 1) * (1 << 18)
    work, _ = work_list(
        jnp.concatenate([ovalue, mvalue], axis=1).reshape(-1),
        jnp.concatenate([ostage, mstage], axis=1).reshape(-1),
    )
    mcuts, mwin, owin = row_of(cuts, q), row_of(starts, q), row_of(starts, q ^ 2)
    info = jnp.concatenate([mcuts, row_of(cuts, q ^ 2), owin, mwin])
    vote = left.astype(jnp.int32)[None]

    def center(group, *marks):
        raw, spans = [], []
        for kind, came, limit in ((0, near, blocks), (1, far, far_blocks)):
            for t in takes[group]:
                if bounds[t] < limit:
                    raw.append(came[t])
                    spans.append((kind, bounds[t], bounds[t + 1] - bounds[t]))
        mine, mark = join((near_mean, far_mean), raw, tuple(spans), *marks)
        return (mine, other_core(mine)), mark

    mark = step(0, mark)
    block_means = bond_means.reshape(blocks, BLOCK)
    block_means, out, send, window, mark = own_stage(
        cfg, info, mlist, work, block_means, xa, xb, mark
    )
    near_mean = from_behind(block_means, "bond", -1)
    far_mean = from_behind(block_means, "bond", -2)
    arrived = {0: other_chip(window)}
    mark = step(1, mark)
    fed, merged = 2, 0
    for group, hop in enumerate(takes):
        while fed < hops and fed <= hop[-1] + 1:
            mark = step(fed, mark, *[arrived[w] for w in SEEN.get(fed, ())])
            fed += 1
        last = group + 1 == len(takes)
        halves, mark = center(group, mark, *([arrived[max(arrived)]] if last else []))
        if fed < hops and len(hop) == 2:
            mark = step(fed, mark, *[arrived[w] for w in SEEN.get(fed, ())])
            fed += 1
        elif last:
            mark = rest(mark)
        merges = tuple(w for w in sorted(arrived) if merged <= w < group or (last and w >= merged))
        merged = max((*merges, merged - 1)) + 1
        out, send, mark, vote, window = halo_stage(
            cfg, group + 1, merges, info, mlist, work, vote, xa, xb, halves,
            [arrived[w] for w in merges], out, send, mark,
        )
        if window is not None:
            arrived[group + 1] = other_chip(window)
    for stride in range((bond_count - 1).bit_length()):
        pairs = [(s, s ^ (1 << stride)) for s in range(bond_count)]
        vote = jnp.maximum(vote, lax.ppermute(vote, "bond", pairs))
    out = merge(cfg, mwin[-2:], mlist, arrived[len(takes)], out)

    trips = (vote[0] + WINDOW - 1) // WINDOW

    def more(state):
        return state[0] < trips

    def turn(state):
        trip, result = state
        at = jnp.minimum(owin[-1] + trip * WINDOW, send.shape[0] - WINDOW)
        got = other_chip(lax.dynamic_slice_in_dim(send, at, WINDOW, axis=0))
        lo = jnp.minimum(mwin[-1] + trip * WINDOW, mcuts[-1])
        hi = jnp.minimum(lo + WINDOW, mcuts[-1])
        return trip + 1, merge(cfg, jnp.stack([lo, hi]), mlist, got, result)

    _, out = lax.while_loop(more, turn, (jnp.int32(0), out))
    return (bond_means, out)


def shards(yields, partners):
    blocks = yields.shape[1] // BLOCK
    snap_count, bond_count = lax.axis_size("snap"), lax.axis_size("bond")
    two_hops = blocks < REACH - 1 <= 2 * blocks
    if (
        two_hops
        and snap_count == 4
        and bond_count & (bond_count - 1) == 0
        and blocks % (2 * CHUNK) == 0
        and blocks // CHUNK >= 4
        and blocks <= 64
        and partners.shape[1] <= 64
        and blocks % PARTS == 0
        and partners.shape[1] % snap_count == 0
        and yields.shape[0] % BLOCK == 0
    ):
        return paired_shards(yields, partners)
    return plain_shards(yields, partners)


def solution(mesh):
    return jax.shard_map(
        shards,
        mesh=mesh,
        in_specs=(P("snap", "bond"), P("bond", None)),
        out_specs=(P("bond"), P("snap", "bond", None, None)),
        check_vma=False,
    )
```

```python
import functools

import jax
import jax.numpy as jnp
from jax import lax
from jax.experimental import pallas as pl
from jax.experimental.pallas import tpu as pltpu
from jax.sharding import PartitionSpec as P

BLOCK = 128
REACH = 56
CHUNK = 4
WINDOW = 16
PARTS = 8
ROOM = 60
UNROLL = 4
CODED = BLOCK + 8
SEEN = {4: (0,), 7: (1,)}
COSTS = (10000, 10000, 10000, 10000, 500, 10000, 500)
TOP = 10.0
F32 = jnp.float32
BF16 = jnp.bfloat16
ANY = pl.BlockSpec(memory_space=pl.ANY)
SMEM = pl.BlockSpec(memory_space=pltpu.SMEM)
VMEM = pl.BlockSpec(memory_space=pltpu.VMEM)


def params(mib):
    return pltpu.CompilerParams(vmem_limit_bytes=mib << 20)


def from_behind(value, axis, steps):
    count = lax.axis_size(axis)
    first, last = (max(0, -steps), min(count, count - steps))
    return lax.ppermute(value, axis, [(source, source + steps) for source in range(first, last)])


def plain_shards(yields, partners):
    snaps_local, columns = yields.shape
    blocks_local = columns // BLOCK
    total_snaps = snaps_local * lax.axis_size("snap")
    local_sums = jnp.sum(yields, axis=0, dtype=F32)
    totals = lax.psum(local_sums, "snap")
    bond_means = totals / total_snaps
    centered = (yields.astype(F32) - bond_means[None, :]).astype(BF16)
    extent = blocks_local + REACH - 1
    hop_count = (extent - 1) // blocks_local
    pieces = [centered]
    for distance in range(1, hop_count + 1):
        kept_blocks = min(blocks_local, extent - distance * blocks_local)
        kept_cols = kept_blocks * BLOCK
        pieces.append(from_behind(centered[:, :kept_cols], "bond", -distance))
    extended = jnp.concatenate(pieces, axis=1).reshape(snaps_local, -1, BLOCK)
    ext_blocks = extended.shape[1]
    first_block = lax.axis_index("bond") * blocks_local
    live_all = partners >= 0
    index_all = jnp.clip(jnp.where(live_all, partners - first_block, 0), 0, ext_blocks - 1)
    inverse = 1.0 / (total_snaps - 1)

    def block_tiles(args):
        block_row, index_row, live_row = args
        own_block = lax.dynamic_index_in_dim(extended, block_row, 1, keepdims=False)
        chosen = jnp.take(extended, index_row, axis=1)
        tile_sum = jnp.einsum("sa,scb->cab", own_block, chosen, preferred_element_type=F32)
        return tile_sum * (live_row.astype(F32) * inverse)[:, None, None]

    per_block = lax.map(
        block_tiles, (jnp.arange(blocks_local, dtype=jnp.int32), index_all, live_all)
    )
    covariance_tiles = lax.psum_scatter(
        jnp.transpose(per_block, (1, 0, 2, 3)), "snap", scatter_dimension=0, tiled=True
    )
    return (bond_means, covariance_tiles)


def cost(micros):
    return pl.CostEstimate(flops=int(micros * 1e9), bytes_accessed=int(micros * 3e6), transcendentals=0)


def token():
    return jax.ShapeDtypeStruct((8, BLOCK), F32)


def feed_kernel(bounds, plan, odd_ref, yields, far, *refs):
    buffers, (in_sems, out_sems) = refs[-2 - len(plan):-2], refs[-2:]
    outs = refs[-3 - 2 * len(plan):-3 - len(plan)]
    odd = odd_ref[0]
    parts = in_sems.shape[1]
    pieces = [(n, r) for r in range(parts) for n in range(len(plan))]

    def span(ref, r):
        rows = ref.shape[0] // parts
        return pl.ds(r * rows, rows)

    def fetch(src, first, n, r):
        rows, wide = span(src, r), buffers[n].shape[1]
        part = src.at[rows, pl.ds(first * BLOCK, wide)]
        return pltpu.make_async_copy(part, buffers[n].at[rows], in_sems.at[n, r])

    def own(n, r):
        return fetch(yields, bounds[plan[n][1]], n, r)

    def relayed(n, r):
        return fetch(far, 0, n, r)

    def store(n, r):
        rows = span(yields, r)
        return pltpu.make_async_copy(buffers[n].at[rows], outs[n].at[rows], out_sems.at[n, r])

    for n, r in pieces:
        if plan[n][0] == "own":
            own(n, r).start()
        else:
            pl.when(odd == 1)(lambda: own(n, r).start())
            pl.when(odd == 0)(lambda: relayed(n, r).start())
    for n, r in pieces:
        own(n, r).wait()
        store(n, r).start()
    for n, r in pieces:
        store(n, r).wait()


def feed(cfg, plan, odd, yields, far, *tokens):
    bounds, parts = cfg["bounds"], 4
    shapes = [(yields.shape[0], (bounds[t + 1] - bounds[t]) * BLOCK) for _, t in plan]
    return pl.pallas_call(
        functools.partial(feed_kernel, bounds, plan),
        in_specs=[SMEM] + [ANY] * (2 + len(tokens)),
        out_specs=[ANY] * (len(plan) + 1),
        out_shape=[jax.ShapeDtypeStruct(shape, BF16) for shape in shapes] + [token()],
        scratch_shapes=[pltpu.VMEM(shape, BF16) for shape in shapes]
        + [pltpu.SemaphoreType.DMA((len(plan), parts))] * 2,
        compiler_params=params(ROOM),
        cost_estimate=cost(COSTS[0]),
        name="feed",
    )(odd, yields, far, *tokens)


def rest_kernel(_, out):
    pass


def rest(after):
    return pl.pallas_call(
        rest_kernel,
        in_specs=[ANY],
        out_specs=ANY,
        out_shape=token(),
        compiler_params=params(ROOM),
        cost_estimate=cost(COSTS[0]),
        name="rest",
    )(after)


def hold_kernel(means, _, out):
    out[...] = means[...]


def held_means(means, after):
    return pl.pallas_call(
        hold_kernel,
        in_specs=[VMEM, ANY],
        out_specs=VMEM,
        out_shape=jax.ShapeDtypeStruct(means.shape, F32),
        compiler_params=params(ROOM),
        cost_estimate=cost(1),
        name="held_means",
    )(means, after)


def sums_kernel(raw_ref, _, out_ref):
    out_ref[0] = jnp.sum(raw_ref[...].astype(F32), axis=0, keepdims=True)


def column_sums(yields, after):
    snaps, columns = yields.shape
    wide = 4 * BLOCK
    steps = columns // wide
    return pl.pallas_call(
        sums_kernel,
        grid=(steps,),
        in_specs=[pl.BlockSpec((snaps, wide), lambda i: (0, i)), ANY],
        out_specs=pl.BlockSpec((1, 1, wide), lambda i: (i, 0, 0)),
        out_shape=jax.ShapeDtypeStruct((steps, 1, wide), F32),
        compiler_params=params(ROOM),
        cost_estimate=cost(COSTS[1]),
        name="column_sums",
    )(yields, after).reshape(columns)


def transpose_kernel(group, raw_ref, mean_ref, out_ref):
    for g in range(group):
        cols = pl.ds(g * BLOCK, BLOCK)
        block = raw_ref[:, cols].astype(F32) - mean_ref[0, :, cols]
        out_ref[g] = block.T.astype(BF16)


def centered_transposed(yields, means):
    snaps, columns = yields.shape
    group = 2
    blocks = columns // BLOCK
    steps = blocks // group
    return pl.pallas_call(
        functools.partial(transpose_kernel, group),
        grid=(steps,),
        in_specs=[
            pl.BlockSpec((snaps, group * BLOCK), lambda i: (0, i)),
            pl.BlockSpec((1, 1, group * BLOCK), lambda i: (i, 0, 0)),
        ],
        out_specs=pl.BlockSpec((group, BLOCK, snaps), lambda i: (i, 0, 0)),
        out_shape=jax.ShapeDtypeStruct((blocks, BLOCK, snaps), BF16),
        compiler_params=params(ROOM),
        cost_estimate=cost(COSTS[2]),
        name="center_transpose",
    )(yields, means.reshape(steps, 1, group * BLOCK))


def entry(entries, n):
    v = entries[n]
    return (v >> 12) & 63, (v >> 8) & 15, v & 255


def travels(entries, n):
    return (entries[n] >> 18) & 1 == 1


def output_place(entries, out, n):
    row, slot, _ = entry(entries, n)
    return out.at[slot, row]


def all_rows(xa, xb, rows_a, rows_b, sems):
    rows = xa.shape[0] // PARTS

    def copies(part):
        span = pl.ds(part * rows, rows)
        return (
            pltpu.make_async_copy(xa.at[span], rows_a.at[span], sems.at[0, part]),
            pltpu.make_async_copy(xb.at[span], rows_b.at[span], sems.at[1, part]),
        )

    def start():
        for part in reversed(range(PARTS)):
            for copy in copies(part):
                copy.start()

    def wait_down_to(here, need):
        for part in reversed(range(PARTS)):

            @pl.when((here > part) & (need <= part))
            def _():
                for copy in copies(part):
                    copy.wait()

        return jnp.minimum(here, need)

    def begin(g, wanted):
        pass

    def ready(g, here, wanted):
        lowest = functools.reduce(jnp.minimum, wanted)
        need = sum(((lowest >= part * rows).astype(jnp.int32) for part in range(1, PARTS)), 0)
        return wait_down_to(here, need)

    def finish(here):
        wait_down_to(here, 0)

    return start, (begin, ready, finish)


def few_rows(xa, xb, rows_a, rows_b, sems):
    def copies(g, wanted):
        for u, row in enumerate(wanted):
            at = (g & 1) * UNROLL + u
            yield pltpu.make_async_copy(xa.at[row], rows_a.at[at], sems.at[0, at])
            yield pltpu.make_async_copy(xb.at[row], rows_b.at[at], sems.at[1, at])

    def begin(g, wanted):
        for copy in copies(g, wanted):
            copy.start()

    def ready(g, here, wanted):
        for copy in copies(g, wanted):
            copy.wait()
        return here

    def finish(here):
        pass

    return begin, ready, finish


def tile_loop(cfg, step, info, work, out, send, stage, store_sem, rows_in, product):
    lo = info[cfg["cut_o"] + step] + info[cfg["cut_m"] + step]
    hi = info[cfg["cut_o"] + step + 1] + info[cfg["cut_m"] + step + 1]
    groups = lax.div(hi - lo + UNROLL - 1, UNROLL)
    begin, ready, finish = rows_in

    def rows_of(g):
        return [entry(work, lo + g * UNROLL + u)[0] for u in range(UNROLL)]

    def each_store(g, act):
        for u in range(UNROLL):
            n, at = lo + g * UNROLL + u, (g & 1) * UNROLL + u
            away = travels(work, n)

            @pl.when((n < hi) & away)
            def _():
                dst = send.at[work[n] >> 19]
                act(pltpu.make_async_copy(stage.at[at], dst, store_sem.at[at]))

            @pl.when((n < hi) & jnp.logical_not(away))
            def _():
                src, dst = stage.at[at, pl.ds(0, BLOCK)], output_place(work, out, n)
                act(pltpu.make_async_copy(src, dst, store_sem.at[at]))

    pl.when(groups > 0)(lambda: begin(0, rows_of(0)))

    def body(g, here):
        base = lo + g * UNROLL
        found = [entry(work, base + u) for u in range(UNROLL)]
        pl.when(g + 1 < groups)(lambda: begin(g + 1, rows_of(g + 1)))
        here = ready(g, here, [row for row, _, _ in found])
        pl.when(g >= 2)(lambda: each_store(g - 2, lambda copy: copy.wait()))
        values = [
            product((g & 1) * UNROLL + u, row, rel) for u, (row, _, rel) in enumerate(found)
        ]
        for u in range(UNROLL):
            at = (g & 1) * UNROLL + u
            top = jnp.maximum(jnp.max(jnp.abs(values[u]), axis=0, keepdims=True), 1e-30)
            power = jnp.where(travels(work, base + u), TOP - jnp.ceil(jnp.log2(top)), 0.0)
            stage[at, 0:BLOCK] = values[u] * jnp.exp2(power)
            stage[at, BLOCK:CODED] = jnp.broadcast_to(power, (CODED - BLOCK, BLOCK))
        each_store(g, lambda copy: copy.start())
        return here

    finish(lax.fori_loop(0, groups, body, jnp.int32(PARTS)))
    pl.when(groups >= 2)(lambda: each_store(groups - 2, lambda copy: copy.wait()))
    pl.when(groups >= 1)(lambda: each_store(groups - 1, lambda copy: copy.wait()))


def send_window(info, at, send, window, sem):
    copy = pltpu.make_async_copy(send.at[pl.ds(info[at], window.shape[0])], window, sem)
    copy.start()
    copy.wait()


def stage_scratch(xa, rows):
    return [
        pltpu.VMEM((rows,) + xa.shape[1:], BF16),
        pltpu.VMEM((rows,) + xa.shape[1:], BF16),
        pltpu.VMEM((2 * UNROLL, CODED, BLOCK), F32),
        pltpu.SemaphoreType.DMA((2, max(PARTS, 2 * UNROLL))),
        pltpu.SemaphoreType.DMA((2 * UNROLL,)),
        pltpu.SemaphoreType.DMA,
    ]


def own_kernel(cfg, info, mlist, work, xa, xb, *refs):
    out, send, window, _, rows_a, rows_b, stage, row_sem, store_sem, sem, zero, zero_sem = refs[
        -12:
    ]
    start_rows, rows_in = all_rows(xa, xb, rows_a, rows_b, row_sem)
    start_rows()

    def product(at, row, rel):
        p = jnp.minimum(rel, xa.shape[0] - 1)
        dims = (((1,), (1,)), ((), ()))
        acc = lax.dot_general(rows_a[row], rows_a[p], dims, preferred_element_type=F32)
        acc += lax.dot_general(rows_b[row], rows_b[p], dims, preferred_element_type=F32)
        return acc * cfg["inverse"]

    zero[...] = jnp.zeros_like(zero)

    def clear(n):
        return pltpu.make_async_copy(zero, output_place(mlist, out, n), zero_sem)

    def start_clear(n, carry):
        clear(n).start()
        return carry

    def wait_clear(n, carry):
        clear(n).wait()
        return carry

    live = info[cfg["cut_m"] + cfg["stages"]]
    tile_loop(cfg, 0, info, work, out, send, stage, store_sem, rows_in, product)
    lax.fori_loop(live, cfg["entries"], start_clear, 0)
    send_window(info, cfg["win_o"], send, window, sem)
    lax.fori_loop(live, cfg["entries"], wait_clear, 0)


def own_stage(cfg, info, mlist, work, xa, xb, *after):
    blocks = xa.shape[0]
    room = max(cfg["windows"] + (WINDOW,))
    return pl.pallas_call(
        functools.partial(own_kernel, cfg),
        in_specs=[SMEM] * 3 + [ANY] * (2 + len(after)),
        out_specs=[ANY, ANY, VMEM, ANY],
        out_shape=[
            jax.ShapeDtypeStruct((cfg["slots"], blocks, BLOCK, BLOCK), F32),
            jax.ShapeDtypeStruct((cfg["entries"] + room, CODED, BLOCK), F32),
            jax.ShapeDtypeStruct((cfg["windows"][0], CODED, BLOCK), F32),
            token(),
        ],
        scratch_shapes=stage_scratch(xa, blocks)
        + [pltpu.VMEM((BLOCK, BLOCK), F32), pltpu.SemaphoreType.DMA],
        compiler_params=params(ROOM),
        cost_estimate=cost(COSTS[3]),
        name="own_tiles",
    )(info, mlist, work, xa, xb, *after)


def merge_parts(cfg, lo, count, mlist, arrived, out, mine, theirs, mine_sem, theirs_sem):
    def read_mine(r):
        src = output_place(mlist, out, lo + r)
        return pltpu.make_async_copy(src, mine.at[r], mine_sem.at[r])

    def read_theirs():
        return pltpu.make_async_copy(arrived, theirs, theirs_sem)

    def write(r):
        dst = output_place(mlist, out, lo + r)
        return pltpu.make_async_copy(mine.at[r], dst, mine_sem.at[r])

    def first(r, carry):
        read_mine(r).start()
        return carry

    def second(r, carry):
        read_mine(r).wait()
        scale = jnp.exp2(-theirs[r, BLOCK:BLOCK + 1])
        mine[r] = mine[r] + theirs[r, 0:BLOCK] * scale
        write(r).start()
        return carry

    def third(r, carry):
        write(r).wait()
        return carry

    def begin():
        read_theirs().start()
        lax.fori_loop(0, count, first, 0)

    def add():
        read_theirs().wait()
        lax.fori_loop(0, count, second, 0)

    return begin, add, lambda: lax.fori_loop(0, count, third, 0)


def merge_scratch(size):
    return [
        pltpu.VMEM((size, BLOCK, BLOCK), F32),
        pltpu.VMEM((size, CODED, BLOCK), F32),
        pltpu.SemaphoreType.DMA((size,)),
        pltpu.SemaphoreType.DMA,
    ]


def join_kernel(spans, *refs):
    kinds = 2 if len(spans) > 0 and any(kind for kind, _, _ in spans) else 1
    means, refs = refs[:kinds], refs[kinds:]
    raw = refs[:len(spans)]
    out, _, rawbuf, done, raw_sem, out_sem = refs[-6:]
    places = [(n, kind, first, j) for n, (kind, first, w) in enumerate(spans) for j in range(w)]

    def fetch(at):
        n, _, _, j = places[at]
        src = raw[n].at[:, pl.ds(j * BLOCK, BLOCK)]
        return pltpu.make_async_copy(src, rawbuf.at[at], raw_sem.at[at])

    def store(at):
        return pltpu.make_async_copy(done.at[at], out.at[at], out_sem.at[at])

    for at in range(len(places)):
        fetch(at).start()
    for at, (_, kind, first, j) in enumerate(places):
        fetch(at).wait()
        block = rawbuf[at].astype(F32) - means[kind][first + j:first + j + 1, :]
        done[at] = block.astype(BF16)
        store(at).start()
    for at in range(len(places)):
        store(at).wait()


def join(means, raw, spans, *after):
    snaps = raw[0].shape[0]
    kinds = 2 if any(kind for kind, _, _ in spans) else 1
    blocks = (sum(w for _, _, w in spans), snaps, BLOCK)
    return pl.pallas_call(
        functools.partial(join_kernel, spans),
        in_specs=[VMEM] * kinds + [ANY] * (len(raw) + len(after)),
        out_specs=[ANY, ANY],
        out_shape=[jax.ShapeDtypeStruct(blocks, BF16), token()],
        scratch_shapes=[
            pltpu.VMEM(blocks, BF16),
            pltpu.VMEM(blocks, BF16),
            pltpu.SemaphoreType.DMA((blocks[0],)),
            pltpu.SemaphoreType.DMA((blocks[0],)),
        ],
        compiler_params=params(ROOM),
        cost_estimate=cost(COSTS[4]),
        name="center_join",
    )(*means[:kinds], *raw, *after)


def halo_kernel(cfg, step, merges, *refs):
    info, mlist, work, cast, xa, xb = refs[:6]
    ca, cb = refs[6:8]
    refs = refs[8:]
    blocks = cfg["blocks"]
    first_block, end_block = cfg["spans"][step - 1]
    arrived, rest = refs[:len(merges)], refs[len(merges):]
    out, send, _, vote = rest[3:7]
    rest = rest[7:]
    if cfg["windows"][step]:
        window, rest = rest[0], rest[1:]
    rows_a, rows_b, stage, row_sem, store_sem, sem, ya, yb, raw_sem = rest[:9]
    vote[0] = cast[0]
    rows_in = few_rows(xa, xb, rows_a, rows_b, row_sem)
    halves = [
        pltpu.make_async_copy(src, dst, raw_sem.at[n])
        for n, (src, dst) in enumerate(((ca, ya), (cb, yb)))
    ]
    for copy in halves:
        copy.start()
    parts = []
    for n, w in enumerate(merges):
        lo = info[cfg["win_m"] + w]
        count = info[cfg["win_m"] + w + 1] - lo
        parts.append(merge_parts(cfg, lo, count, mlist, arrived[n], out, *rest[9 + 4 * n:13 + 4 * n]))
    for first, _, _ in parts:
        first()
    for copy in halves:
        copy.wait()

    def product(at, row, rel):
        near = rel - blocks - first_block
        far = rel - 2 * blocks - first_block + end_block - first_block
        j = jnp.clip(jnp.where(rel >= 2 * blocks, far, near), 0, ya.shape[0] - 1)
        acc = jnp.dot(rows_a[at], ya[j], preferred_element_type=F32)
        acc += jnp.dot(rows_b[at], yb[j], preferred_element_type=F32)
        return acc * cfg["inverse"]

    tile_loop(cfg, step, info, work, out, send, stage, store_sem, rows_in, product)
    for _, second, _ in parts:
        second()
    if cfg["windows"][step]:
        send_window(info, cfg["win_o"] + step, send, window, sem)
    for _, _, third in parts:
        third()


def halo_stage(cfg, step, merges, info, mlist, work, cast, xa, xb, halves, arrived, out, send, after):
    count = 6 + len(halves) + len(arrived)
    size = cfg["windows"][step]
    shapes = [
        jax.ShapeDtypeStruct(out.shape, F32),
        jax.ShapeDtypeStruct(send.shape, F32),
        token(),
        jax.ShapeDtypeStruct((1,), jnp.int32),
        jax.ShapeDtypeStruct((size, CODED, BLOCK), F32),
    ]
    scratch = stage_scratch(xa, 2 * UNROLL) + [
        pltpu.VMEM(halves[0].shape[-3:], BF16),
        pltpu.VMEM(halves[0].shape[-3:], BF16),
        pltpu.SemaphoreType.DMA((2,)),
    ]
    for window in arrived:
        scratch += merge_scratch(window.shape[0])
    made = pl.pallas_call(
        functools.partial(halo_kernel, cfg, step, merges),
        in_specs=[SMEM] * 4 + [ANY] * (count - 1),
        out_specs=[ANY, ANY, ANY, SMEM, VMEM][:5 if size else 4],
        out_shape=shapes[:5 if size else 4],
        scratch_shapes=scratch,
        input_output_aliases={count: 0, count + 1: 1},
        compiler_params=params(ROOM),
        cost_estimate=cost(COSTS[5]),
        name="halo_tiles",
    )(info, mlist, work, cast, xa, xb, *halves, *arrived, out, send, after)
    return made if size else (*made, None)


def merge_kernel(cfg, span, mlist, arrived, _, out, *scratch):
    lo = span[0]
    for part in merge_parts(cfg, lo, span[1] - lo, mlist, arrived, out, *scratch):
        part()


def merge(cfg, span, mlist, arrived, out):
    return pl.pallas_call(
        functools.partial(merge_kernel, cfg),
        in_specs=[SMEM, SMEM, ANY, ANY],
        out_specs=ANY,
        out_shape=jax.ShapeDtypeStruct(out.shape, F32),
        scratch_shapes=merge_scratch(arrived.shape[0]),
        input_output_aliases={3: 0},
        compiler_params=params(ROOM),
        cost_estimate=cost(COSTS[6]),
        name="merge_tiles",
    )(span, mlist, arrived, out)


def work_list(value, stage):
    entries = value.size
    ids = jnp.arange(entries, dtype=jnp.int32)
    key = (stage + 1) * entries - ids
    rank = jnp.sum((key[None, :] < key[:, None]).astype(jnp.int32), axis=1).astype(jnp.int32)
    ordered = jnp.sum(jnp.where(rank[None, :] == ids[:, None], value[None, :], 0), axis=1)
    return jnp.pad(ordered.astype(jnp.int32), (0, UNROLL)), rank


def window_starts(cuts, sizes):
    sent = jnp.array([sum(sizes[:w]) for w in range(len(sizes) + 1)], jnp.int32)
    later = sent[:, None] - sent[None, :]
    reach = jnp.where(later >= 0, cuts[..., None, :] + later, jnp.int32(1 << 30))
    return jnp.min(reach, axis=-1).astype(jnp.int32)


def hop_plan(blocks):
    hops = blocks // CHUNK
    stages = [(t, t + 1) for t in range(0, hops, 2)]
    return tuple(range(0, blocks + 1, CHUNK)), tuple(stages)


def paired_shards(yields, partners):
    snaps_local, columns = yields.shape
    blocks = columns // BLOCK
    snap_count, bond_count = lax.axis_size("snap"), lax.axis_size("bond")
    total_snaps = snaps_local * snap_count
    q, d = lax.axis_index("snap"), lax.axis_index("bond")
    odd = lax.rem(d, 2).astype(jnp.int32)[None]
    slots = partners.shape[1] // snap_count
    bounds, takes = hop_plan(blocks)
    hops = len(bounds) - 1
    far_blocks = REACH - 1 - blocks
    stages = len(takes) + 1
    windows = (3 * WINDOW, WINDOW + 8) + (2 * WINDOW, WINDOW + 8, WINDOW + 8)
    cfg = {
        "entries": blocks * slots,
        "spans": tuple((bounds[hop[0]], bounds[hop[-1] + 1]) for hop in takes),
        "slots": slots,
        "blocks": blocks,
        "bounds": bounds,
        "windows": windows,
        "stages": stages,
        "cut_m": 0,
        "cut_o": stages + 1,
        "win_o": 2 * (stages + 1),
        "win_m": 3 * (stages + 1),
        "inverse": 1.0 / (total_snaps - 1),
    }

    def other_core(value):
        return lax.ppermute(value, "snap", [(s, s ^ 1) for s in range(snap_count)])

    def across(value):
        return lax.ppermute(value, "snap", [(s, s ^ 2) for s in range(snap_count)])

    def other_chip(value):
        return across(value.astype(jnp.float16)).astype(F32)

    far, near = [None] * hops, [None] * hops

    def send_far(t, value):
        far[t] = lax.ppermute(value, "bond", [(s, s - 2) for s in range(2, bond_count)])

    def send_near(t, value):
        near[t] = lax.ppermute(value, "bond", [(s, s ^ 1) for s in range(bond_count)])

    second, mark = feed(cfg, (("own", 1),), odd, yields, yields)
    send_far(1, second)
    first, mark = feed(cfg, (("own", 0),), odd, yields, yields, mark)
    send_far(0, first)

    def step(t, *marks):
        plan = (("pick", t),)
        if t < hops - 2:
            plan += (("own", t + 2),)
        made = feed(cfg, plan, odd, yields, far[t], *marks)
        send_near(t, made[0])
        if len(plan) == 2:
            send_far(t + 2, made[1])
        return made[-1]

    sums = column_sums(yields, mark)
    sums = sums + other_core(sums)
    totals = sums + across(sums)
    bond_means = totals / total_snaps
    xa = centered_transposed(yields, bond_means)
    xb = other_core(xa)

    rel = partners - d * blocks
    live = partners >= 0
    halo_block = jnp.where(rel < 2 * blocks, rel - blocks, rel - 2 * blocks)
    ends = jnp.array([end for _, end in cfg["spans"][:-1]], jnp.int32)
    taken = jnp.sum((halo_block[..., None] >= ends).astype(jnp.int32), axis=-1)
    stage = jnp.where(live, jnp.where(rel < blocks, 0, taken + 1), stages)
    groups = stage.reshape(blocks, snap_count, slots)
    marks = jnp.arange(stages + 1, dtype=jnp.int32)
    cuts = jnp.sum((groups[..., None] < marks).astype(jnp.int32), axis=(0, 2))
    starts = window_starts(cuts, windows)
    left = jnp.max(cuts[:, -1] - starts[:, -1])

    def row_of(table, owner):
        return lax.dynamic_index_in_dim(table, owner, 0, keepdims=False)

    def listed(owner):
        def cut(a):
            return lax.dynamic_slice_in_dim(a, owner * slots, slots, axis=1)

        rows = lax.broadcasted_iota(jnp.int32, (blocks, slots), 0)
        value = rows * 4096 + lax.broadcasted_iota(jnp.int32, (blocks, slots), 1) * 256
        value, when = value + cut(jnp.where(live, rel, 0)), cut(stage)
        ordered, rank = work_list(value.reshape(-1), when.reshape(-1))
        return value, when, ordered, rank.reshape(blocks, slots)

    mvalue, mstage, mlist, _ = listed(q)
    ovalue, ostage, _, orank = listed(q ^ 2)
    ovalue = ovalue + (2 * orank + 1) * (1 << 18)
    work, _ = work_list(
        jnp.concatenate([ovalue, mvalue], axis=1).reshape(-1),
        jnp.concatenate([ostage, mstage], axis=1).reshape(-1),
    )
    mcuts, mwin, owin = row_of(cuts, q), row_of(starts, q), row_of(starts, q ^ 2)
    info = jnp.concatenate([mcuts, row_of(cuts, q ^ 2), owin, mwin])
    vote = left.astype(jnp.int32)[None]

    def center(group, *marks):
        raw, spans = [], []
        for kind, came, limit in ((0, near, blocks), (1, far, far_blocks)):
            for t in takes[group]:
                if bounds[t] < limit:
                    raw.append(came[t])
                    spans.append((kind, bounds[t], bounds[t + 1] - bounds[t]))
        mine, mark = join((near_mean, far_mean), raw, tuple(spans), *marks)
        return (mine, other_core(mine)), mark

    mark = step(0, mark)
    mark = step(1, mark)
    block_means = bond_means.reshape(blocks, BLOCK)
    out, send, window, mark = own_stage(cfg, info, mlist, work, xa, xb, mark)
    mark = step(2, mark)
    block_means = held_means(block_means, mark)
    near_mean = from_behind(block_means, "bond", -1)
    far_mean = from_behind(block_means, "bond", -2)
    arrived = {0: other_chip(window)}
    fed, merged = 3, 0
    for group, hop in enumerate(takes):
        while fed < hops and fed <= hop[-1] + 1:
            mark = step(fed, mark, *[arrived[w] for w in SEEN.get(fed, ())])
            fed += 1
        last = group + 1 == len(takes)
        halves, mark = center(group, mark)
        if fed < hops and len(hop) == 2:
            mark = step(fed, mark, *[arrived[w] for w in SEEN.get(fed, ())])
            fed += 1
        elif last:
            mark = rest(mark)
        merges = tuple(w for w in sorted(arrived) if merged <= w < group)
        merged = max((*merges, merged - 1)) + 1
        out, send, mark, vote, window = halo_stage(
            cfg, group + 1, merges, info, mlist, work, vote, xa, xb, halves,
            [arrived[w] for w in merges], out, send, mark,
        )
        if window is not None:
            arrived[group + 1] = other_chip(window)
    for stride in range((bond_count - 1).bit_length()):
        pairs = [(s, s ^ (1 << stride)) for s in range(bond_count)]
        vote = jnp.maximum(vote, lax.ppermute(vote, "bond", pairs))
    for w in sorted(arrived):
        if w >= merged:
            out = merge(cfg, mwin[w : w + 2], mlist, arrived[w], out)

    trips = (vote[0] + WINDOW - 1) // WINDOW

    def more(state):
        return state[0] < trips

    def turn(state):
        trip, result = state
        at = jnp.minimum(owin[-1] + trip * WINDOW, send.shape[0] - WINDOW)
        got = other_chip(lax.dynamic_slice_in_dim(send, at, WINDOW, axis=0))
        lo = jnp.minimum(mwin[-1] + trip * WINDOW, mcuts[-1])
        hi = jnp.minimum(lo + WINDOW, mcuts[-1])
        return trip + 1, merge(cfg, jnp.stack([lo, hi]), mlist, got, result)

    _, out = lax.while_loop(more, turn, (jnp.int32(0), out))
    return (bond_means, out)


def shards(yields, partners):
    blocks = yields.shape[1] // BLOCK
    snap_count, bond_count = lax.axis_size("snap"), lax.axis_size("bond")
    two_hops = blocks < REACH - 1 <= 2 * blocks
    if (
        two_hops
        and snap_count == 4
        and bond_count & (bond_count - 1) == 0
        and blocks % (2 * CHUNK) == 0
        and blocks // CHUNK >= 4
        and blocks <= 64
        and partners.shape[1] <= 64
        and blocks % PARTS == 0
        and partners.shape[1] % snap_count == 0
        and yields.shape[0] % BLOCK == 0
    ):
        return paired_shards(yields, partners)
    return plain_shards(yields, partners)


def solution(mesh):
    return jax.shard_map(
        shards,
        mesh=mesh,
        in_specs=(P("snap", "bond"), P("bond", None)),
        out_specs=(P("bond"), P("snap", "bond", None, None)),
        check_vma=False,
    )
```

```python
import functools

import jax
import jax.numpy as jnp
from jax import lax
from jax.experimental import pallas as pl
from jax.experimental.pallas import tpu as pltpu
from jax.sharding import PartitionSpec as P

BLOCK = 128
REACH = 56
CHUNK = 4
WINDOW = 16
PARTS = 8
ROOM = 60
UNROLL = 4
CODED = BLOCK + 8
SEEN = {4: (0,), 7: (1,)}
COSTS = (10000, 10000, 10000, 10000, 500, 10000, 500)
TOP = 10.0
F32 = jnp.float32
BF16 = jnp.bfloat16
ANY = pl.BlockSpec(memory_space=pl.ANY)
SMEM = pl.BlockSpec(memory_space=pltpu.SMEM)
VMEM = pl.BlockSpec(memory_space=pltpu.VMEM)


def params(mib):
    return pltpu.CompilerParams(vmem_limit_bytes=mib << 20)


def from_behind(value, axis, steps):
    count = lax.axis_size(axis)
    first, last = (max(0, -steps), min(count, count - steps))
    return lax.ppermute(value, axis, [(source, source + steps) for source in range(first, last)])


def plain_shards(yields, partners):
    snaps_local, columns = yields.shape
    blocks_local = columns // BLOCK
    total_snaps = snaps_local * lax.axis_size("snap")
    local_sums = jnp.sum(yields, axis=0, dtype=F32)
    totals = lax.psum(local_sums, "snap")
    bond_means = totals / total_snaps
    centered = (yields.astype(F32) - bond_means[None, :]).astype(BF16)
    extent = blocks_local + REACH - 1
    hop_count = (extent - 1) // blocks_local
    pieces = [centered]
    for distance in range(1, hop_count + 1):
        kept_blocks = min(blocks_local, extent - distance * blocks_local)
        kept_cols = kept_blocks * BLOCK
        pieces.append(from_behind(centered[:, :kept_cols], "bond", -distance))
    extended = jnp.concatenate(pieces, axis=1).reshape(snaps_local, -1, BLOCK)
    ext_blocks = extended.shape[1]
    first_block = lax.axis_index("bond") * blocks_local
    live_all = partners >= 0
    index_all = jnp.clip(jnp.where(live_all, partners - first_block, 0), 0, ext_blocks - 1)
    inverse = 1.0 / (total_snaps - 1)

    def block_tiles(args):
        block_row, index_row, live_row = args
        own_block = lax.dynamic_index_in_dim(extended, block_row, 1, keepdims=False)
        chosen = jnp.take(extended, index_row, axis=1)
        tile_sum = jnp.einsum("sa,scb->cab", own_block, chosen, preferred_element_type=F32)
        return tile_sum * (live_row.astype(F32) * inverse)[:, None, None]

    per_block = lax.map(
        block_tiles, (jnp.arange(blocks_local, dtype=jnp.int32), index_all, live_all)
    )
    covariance_tiles = lax.psum_scatter(
        jnp.transpose(per_block, (1, 0, 2, 3)), "snap", scatter_dimension=0, tiled=True
    )
    return (bond_means, covariance_tiles)


def cost(micros):
    return pl.CostEstimate(flops=int(micros * 1e9), bytes_accessed=int(micros * 3e6), transcendentals=0)


def token():
    return jax.ShapeDtypeStruct((8, BLOCK), F32)


def feed_kernel(bounds, plan, odd_ref, yields, far, *refs):
    buffers, (in_sems, out_sems) = refs[-2 - len(plan):-2], refs[-2:]
    outs = refs[-3 - 2 * len(plan):-3 - len(plan)]
    odd = odd_ref[0]
    parts = in_sems.shape[1]
    pieces = [(n, r) for r in range(parts) for n in range(len(plan))]

    def span(ref, r):
        rows = ref.shape[0] // parts
        return pl.ds(r * rows, rows)

    def fetch(src, first, n, r):
        rows, wide = span(src, r), buffers[n].shape[1]
        part = src.at[rows, pl.ds(first * BLOCK, wide)]
        return pltpu.make_async_copy(part, buffers[n].at[rows], in_sems.at[n, r])

    def own(n, r):
        return fetch(yields, bounds[plan[n][1]], n, r)

    def relayed(n, r):
        return fetch(far, 0, n, r)

    def store(n, r):
        rows = span(yields, r)
        return pltpu.make_async_copy(buffers[n].at[rows], outs[n].at[rows], out_sems.at[n, r])

    for n, r in pieces:
        if plan[n][0] == "own":
            own(n, r).start()
        else:
            pl.when(odd == 1)(lambda: own(n, r).start())
            pl.when(odd == 0)(lambda: relayed(n, r).start())
    for n, r in pieces:
        own(n, r).wait()
        store(n, r).start()
    for n, r in pieces:
        store(n, r).wait()


def feed(cfg, plan, odd, yields, far, *tokens):
    bounds, parts = cfg["bounds"], 4
    shapes = [(yields.shape[0], (bounds[t + 1] - bounds[t]) * BLOCK) for _, t in plan]
    return pl.pallas_call(
        functools.partial(feed_kernel, bounds, plan),
        in_specs=[SMEM] + [ANY] * (2 + len(tokens)),
        out_specs=[ANY] * (len(plan) + 1),
        out_shape=[jax.ShapeDtypeStruct(shape, BF16) for shape in shapes] + [token()],
        scratch_shapes=[pltpu.VMEM(shape, BF16) for shape in shapes]
        + [pltpu.SemaphoreType.DMA((len(plan), parts))] * 2,
        compiler_params=params(ROOM),
        cost_estimate=cost(COSTS[0]),
        name="feed",
    )(odd, yields, far, *tokens)


def rest_kernel(_, out):
    pass


def rest(after):
    return pl.pallas_call(
        rest_kernel,
        in_specs=[ANY],
        out_specs=ANY,
        out_shape=token(),
        compiler_params=params(ROOM),
        cost_estimate=cost(COSTS[0]),
        name="rest",
    )(after)


def hold_kernel(means, _, out):
    out[...] = means[...]


def held_means(means, after):
    return pl.pallas_call(
        hold_kernel,
        in_specs=[VMEM, ANY],
        out_specs=VMEM,
        out_shape=jax.ShapeDtypeStruct(means.shape, F32),
        compiler_params=params(ROOM),
        cost_estimate=cost(1),
        name="held_means",
    )(means, after)


def sums_kernel(raw_ref, _, out_ref):
    out_ref[0] = jnp.sum(raw_ref[...].astype(F32), axis=0, keepdims=True)


def column_sums(yields, after):
    snaps, columns = yields.shape
    wide = 4 * BLOCK
    steps = columns // wide
    return pl.pallas_call(
        sums_kernel,
        grid=(steps,),
        in_specs=[pl.BlockSpec((snaps, wide), lambda i: (0, i)), ANY],
        out_specs=pl.BlockSpec((1, 1, wide), lambda i: (i, 0, 0)),
        out_shape=jax.ShapeDtypeStruct((steps, 1, wide), F32),
        compiler_params=params(ROOM),
        cost_estimate=cost(COSTS[1]),
        name="column_sums",
    )(yields, after).reshape(columns)


def transpose_kernel(group, raw_ref, mean_ref, out_ref):
    for g in range(group):
        cols = pl.ds(g * BLOCK, BLOCK)
        block = raw_ref[:, cols].astype(F32) - mean_ref[0, :, cols]
        out_ref[g] = block.T.astype(BF16)


def centered_transposed(yields, means):
    snaps, columns = yields.shape
    group = 2
    blocks = columns // BLOCK
    steps = blocks // group
    return pl.pallas_call(
        functools.partial(transpose_kernel, group),
        grid=(steps,),
        in_specs=[
            pl.BlockSpec((snaps, group * BLOCK), lambda i: (0, i)),
            pl.BlockSpec((1, 1, group * BLOCK), lambda i: (i, 0, 0)),
        ],
        out_specs=pl.BlockSpec((group, BLOCK, snaps), lambda i: (i, 0, 0)),
        out_shape=jax.ShapeDtypeStruct((blocks, BLOCK, snaps), BF16),
        compiler_params=params(ROOM),
        cost_estimate=cost(COSTS[2]),
        name="center_transpose",
    )(yields, means.reshape(steps, 1, group * BLOCK))


def entry(entries, n):
    v = entries[n]
    return (v >> 12) & 63, (v >> 8) & 15, v & 255


def travels(entries, n):
    return (entries[n] >> 18) & 1 == 1


def output_place(entries, out, n):
    row, slot, _ = entry(entries, n)
    return out.at[slot, row]


def all_rows(xa, xb, rows_a, rows_b, sems):
    rows = xa.shape[0] // PARTS

    def copies(part):
        span = pl.ds(part * rows, rows)
        return (
            pltpu.make_async_copy(xa.at[span], rows_a.at[span], sems.at[0, part]),
            pltpu.make_async_copy(xb.at[span], rows_b.at[span], sems.at[1, part]),
        )

    def start():
        for part in reversed(range(PARTS)):
            for copy in copies(part):
                copy.start()

    def wait_down_to(here, need):
        for part in reversed(range(PARTS)):

            @pl.when((here > part) & (need <= part))
            def _():
                for copy in copies(part):
                    copy.wait()

        return jnp.minimum(here, need)

    def begin(g, wanted):
        pass

    def ready(g, here, wanted):
        lowest = functools.reduce(jnp.minimum, wanted)
        need = sum(((lowest >= part * rows).astype(jnp.int32) for part in range(1, PARTS)), 0)
        return wait_down_to(here, need)

    def finish(here):
        wait_down_to(here, 0)

    return start, (begin, ready, finish)


def few_rows(xa, xb, rows_a, rows_b, sems):
    def copies(g, wanted):
        for u, row in enumerate(wanted):
            at = (g & 1) * UNROLL + u
            yield pltpu.make_async_copy(xa.at[row], rows_a.at[at], sems.at[0, at])
            yield pltpu.make_async_copy(xb.at[row], rows_b.at[at], sems.at[1, at])

    def begin(g, wanted):
        for copy in copies(g, wanted):
            copy.start()

    def ready(g, here, wanted):
        for copy in copies(g, wanted):
            copy.wait()
        return here

    def finish(here):
        pass

    return begin, ready, finish


def tile_loop(cfg, step, info, work, out, send, stage, store_sem, rows_in, product):
    lo = info[cfg["cut_o"] + step] + info[cfg["cut_m"] + step]
    hi = info[cfg["cut_o"] + step + 1] + info[cfg["cut_m"] + step + 1]
    groups = lax.div(hi - lo + UNROLL - 1, UNROLL)
    begin, ready, finish = rows_in

    def rows_of(g):
        return [entry(work, lo + g * UNROLL + u)[0] for u in range(UNROLL)]

    def each_store(g, act):
        for u in range(UNROLL):
            n, at = lo + g * UNROLL + u, (g & 1) * UNROLL + u
            away = travels(work, n)

            @pl.when((n < hi) & away)
            def _():
                dst = send.at[work[n] >> 19]
                act(pltpu.make_async_copy(stage.at[at], dst, store_sem.at[at]))

            @pl.when((n < hi) & jnp.logical_not(away))
            def _():
                src, dst = stage.at[at, pl.ds(0, BLOCK)], output_place(work, out, n)
                act(pltpu.make_async_copy(src, dst, store_sem.at[at]))

    pl.when(groups > 0)(lambda: begin(0, rows_of(0)))

    def body(g, here):
        base = lo + g * UNROLL
        found = [entry(work, base + u) for u in range(UNROLL)]
        pl.when(g + 1 < groups)(lambda: begin(g + 1, rows_of(g + 1)))
        here = ready(g, here, [row for row, _, _ in found])
        pl.when(g >= 2)(lambda: each_store(g - 2, lambda copy: copy.wait()))
        values = [
            product((g & 1) * UNROLL + u, row, rel) for u, (row, _, rel) in enumerate(found)
        ]
        for u in range(UNROLL):
            at = (g & 1) * UNROLL + u
            top = jnp.maximum(jnp.max(jnp.abs(values[u]), axis=0, keepdims=True), 1e-30)
            power = jnp.where(travels(work, base + u), TOP - jnp.ceil(jnp.log2(top)), 0.0)
            stage[at, 0:BLOCK] = values[u] * jnp.exp2(power)
            stage[at, BLOCK:CODED] = jnp.broadcast_to(power, (CODED - BLOCK, BLOCK))
        each_store(g, lambda copy: copy.start())
        return here

    finish(lax.fori_loop(0, groups, body, jnp.int32(PARTS)))
    pl.when(groups >= 2)(lambda: each_store(groups - 2, lambda copy: copy.wait()))
    pl.when(groups >= 1)(lambda: each_store(groups - 1, lambda copy: copy.wait()))


def send_window(info, at, send, window, sem):
    copy = pltpu.make_async_copy(send.at[pl.ds(info[at], window.shape[0])], window, sem)
    copy.start()
    copy.wait()


def stage_scratch(xa, rows):
    return [
        pltpu.VMEM((rows,) + xa.shape[1:], BF16),
        pltpu.VMEM((rows,) + xa.shape[1:], BF16),
        pltpu.VMEM((2 * UNROLL, CODED, BLOCK), F32),
        pltpu.SemaphoreType.DMA((2, max(PARTS, 2 * UNROLL))),
        pltpu.SemaphoreType.DMA((2 * UNROLL,)),
        pltpu.SemaphoreType.DMA,
    ]


def own_kernel(cfg, info, mlist, work, xa, xb, *refs):
    out, send, window, _, rows_a, rows_b, stage, row_sem, store_sem, sem, zero, zero_sem = refs[
        -12:
    ]
    start_rows, rows_in = all_rows(xa, xb, rows_a, rows_b, row_sem)
    start_rows()

    def product(at, row, rel):
        p = jnp.minimum(rel, xa.shape[0] - 1)
        dims = (((1,), (1,)), ((), ()))
        acc = lax.dot_general(rows_a[row], rows_a[p], dims, preferred_element_type=F32)
        acc += lax.dot_general(rows_b[row], rows_b[p], dims, preferred_element_type=F32)
        return acc * cfg["inverse"]

    zero[...] = jnp.zeros_like(zero)

    def clear(n):
        return pltpu.make_async_copy(zero, output_place(mlist, out, n), zero_sem)

    def start_clear(n, carry):
        clear(n).start()
        return carry

    def wait_clear(n, carry):
        clear(n).wait()
        return carry

    live = info[cfg["cut_m"] + cfg["stages"]]
    tile_loop(cfg, 0, info, work, out, send, stage, store_sem, rows_in, product)
    lax.fori_loop(live, cfg["entries"], start_clear, 0)
    send_window(info, cfg["win_o"], send, window, sem)
    lax.fori_loop(live, cfg["entries"], wait_clear, 0)


def own_stage(cfg, info, mlist, work, xa, xb, *after):
    blocks = xa.shape[0]
    room = max(cfg["windows"] + (WINDOW,))
    return pl.pallas_call(
        functools.partial(own_kernel, cfg),
        in_specs=[SMEM] * 3 + [ANY] * (2 + len(after)),
        out_specs=[ANY, ANY, VMEM, ANY],
        out_shape=[
            jax.ShapeDtypeStruct((cfg["slots"], blocks, BLOCK, BLOCK), F32),
            jax.ShapeDtypeStruct((cfg["entries"] + room, CODED, BLOCK), F32),
            jax.ShapeDtypeStruct((cfg["windows"][0], CODED, BLOCK), F32),
            token(),
        ],
        scratch_shapes=stage_scratch(xa, blocks)
        + [pltpu.VMEM((BLOCK, BLOCK), F32), pltpu.SemaphoreType.DMA],
        compiler_params=params(ROOM),
        cost_estimate=cost(COSTS[3]),
        name="own_tiles",
    )(info, mlist, work, xa, xb, *after)


def merge_parts(cfg, lo, count, mlist, arrived, out, mine, theirs, mine_sem, theirs_sem):
    def read_mine(r):
        src = output_place(mlist, out, lo + r)
        return pltpu.make_async_copy(src, mine.at[r], mine_sem.at[r])

    def read_theirs():
        return pltpu.make_async_copy(arrived, theirs, theirs_sem)

    def write(r):
        dst = output_place(mlist, out, lo + r)
        return pltpu.make_async_copy(mine.at[r], dst, mine_sem.at[r])

    def first(r, carry):
        read_mine(r).start()
        return carry

    def second(r, carry):
        read_mine(r).wait()
        scale = jnp.exp2(-theirs[r, BLOCK:BLOCK + 1])
        mine[r] = mine[r] + theirs[r, 0:BLOCK] * scale
        write(r).start()
        return carry

    def third(r, carry):
        write(r).wait()
        return carry

    def begin():
        read_theirs().start()
        lax.fori_loop(0, count, first, 0)

    def add():
        read_theirs().wait()
        lax.fori_loop(0, count, second, 0)

    return begin, add, lambda: lax.fori_loop(0, count, third, 0)


def merge_scratch(size):
    return [
        pltpu.VMEM((size, BLOCK, BLOCK), F32),
        pltpu.VMEM((size, CODED, BLOCK), F32),
        pltpu.SemaphoreType.DMA((size,)),
        pltpu.SemaphoreType.DMA,
    ]


def join_kernel(spans, *refs):
    kinds = 2 if len(spans) > 0 and any(kind for kind, _, _ in spans) else 1
    means, refs = refs[:kinds], refs[kinds:]
    raw = refs[:len(spans)]
    out, _, rawbuf, done, raw_sem, out_sem = refs[-6:]
    places = [(n, kind, first, j) for n, (kind, first, w) in enumerate(spans) for j in range(w)]

    def fetch(at):
        n, _, _, j = places[at]
        src = raw[n].at[:, pl.ds(j * BLOCK, BLOCK)]
        return pltpu.make_async_copy(src, rawbuf.at[at], raw_sem.at[at])

    def store(at):
        return pltpu.make_async_copy(done.at[at], out.at[at], out_sem.at[at])

    for at in range(len(places)):
        fetch(at).start()
    for at, (_, kind, first, j) in enumerate(places):
        fetch(at).wait()
        block = rawbuf[at].astype(F32) - means[kind][first + j:first + j + 1, :]
        done[at] = block.astype(BF16)
        store(at).start()
    for at in range(len(places)):
        store(at).wait()


def join(means, raw, spans, *after):
    snaps = raw[0].shape[0]
    kinds = 2 if any(kind for kind, _, _ in spans) else 1
    blocks = (sum(w for _, _, w in spans), snaps, BLOCK)
    return pl.pallas_call(
        functools.partial(join_kernel, spans),
        in_specs=[VMEM] * kinds + [ANY] * (len(raw) + len(after)),
        out_specs=[ANY, ANY],
        out_shape=[jax.ShapeDtypeStruct(blocks, BF16), token()],
        scratch_shapes=[
            pltpu.VMEM(blocks, BF16),
            pltpu.VMEM(blocks, BF16),
            pltpu.SemaphoreType.DMA((blocks[0],)),
            pltpu.SemaphoreType.DMA((blocks[0],)),
        ],
        compiler_params=params(ROOM),
        cost_estimate=cost(COSTS[4]),
        name="center_join",
    )(*means[:kinds], *raw, *after)


def halo_kernel(cfg, step, merges, *refs):
    info, mlist, work, cast, xa, xb = refs[:6]
    ca, cb = refs[6:8]
    refs = refs[8:]
    blocks = cfg["blocks"]
    first_block, end_block = cfg["spans"][step - 1]
    arrived, rest = refs[:len(merges)], refs[len(merges):]
    out, send, _, vote = rest[3:7]
    rest = rest[7:]
    if cfg["windows"][step]:
        window, rest = rest[0], rest[1:]
    rows_a, rows_b, stage, row_sem, store_sem, sem, ya, yb, raw_sem = rest[:9]
    vote[0] = cast[0]
    rows_in = few_rows(xa, xb, rows_a, rows_b, row_sem)
    halves = [
        pltpu.make_async_copy(src, dst, raw_sem.at[n])
        for n, (src, dst) in enumerate(((ca, ya), (cb, yb)))
    ]
    for copy in halves:
        copy.start()
    parts = []
    for n, w in enumerate(merges):
        lo = info[cfg["win_m"] + w]
        count = info[cfg["win_m"] + w + 1] - lo
        parts.append(merge_parts(cfg, lo, count, mlist, arrived[n], out, *rest[9 + 4 * n:13 + 4 * n]))
    for first, _, _ in parts:
        first()
    for copy in halves:
        copy.wait()

    def product(at, row, rel):
        near = rel - blocks - first_block
        far = rel - 2 * blocks - first_block + end_block - first_block
        j = jnp.clip(jnp.where(rel >= 2 * blocks, far, near), 0, ya.shape[0] - 1)
        acc = jnp.dot(rows_a[at], ya[j], preferred_element_type=F32)
        acc += jnp.dot(rows_b[at], yb[j], preferred_element_type=F32)
        return acc * cfg["inverse"]

    tile_loop(cfg, step, info, work, out, send, stage, store_sem, rows_in, product)
    for _, second, _ in parts:
        second()
    if cfg["windows"][step]:
        send_window(info, cfg["win_o"] + step, send, window, sem)
    for _, _, third in parts:
        third()


def halo_stage(cfg, step, merges, info, mlist, work, cast, xa, xb, halves, arrived, out, send, after):
    count = 6 + len(halves) + len(arrived)
    size = cfg["windows"][step]
    shapes = [
        jax.ShapeDtypeStruct(out.shape, F32),
        jax.ShapeDtypeStruct(send.shape, F32),
        token(),
        jax.ShapeDtypeStruct((1,), jnp.int32),
        jax.ShapeDtypeStruct((size, CODED, BLOCK), F32),
    ]
    scratch = stage_scratch(xa, 2 * UNROLL) + [
        pltpu.VMEM(halves[0].shape[-3:], BF16),
        pltpu.VMEM(halves[0].shape[-3:], BF16),
        pltpu.SemaphoreType.DMA((2,)),
    ]
    for window in arrived:
        scratch += merge_scratch(window.shape[0])
    made = pl.pallas_call(
        functools.partial(halo_kernel, cfg, step, merges),
        in_specs=[SMEM] * 4 + [ANY] * (count - 1),
        out_specs=[ANY, ANY, ANY, SMEM, VMEM][:5 if size else 4],
        out_shape=shapes[:5 if size else 4],
        scratch_shapes=scratch,
        input_output_aliases={count: 0, count + 1: 1},
        compiler_params=params(ROOM),
        cost_estimate=cost(COSTS[5]),
        name="halo_tiles",
    )(info, mlist, work, cast, xa, xb, *halves, *arrived, out, send, after)
    return made if size else (*made, None)


def merge_kernel(cfg, span, mlist, arrived, _, out, *scratch):
    lo = span[0]
    for part in merge_parts(cfg, lo, span[1] - lo, mlist, arrived, out, *scratch):
        part()


def merge(cfg, span, mlist, arrived, out):
    return pl.pallas_call(
        functools.partial(merge_kernel, cfg),
        in_specs=[SMEM, SMEM, ANY, ANY],
        out_specs=ANY,
        out_shape=jax.ShapeDtypeStruct(out.shape, F32),
        scratch_shapes=merge_scratch(arrived.shape[0]),
        input_output_aliases={3: 0},
        compiler_params=params(ROOM),
        cost_estimate=cost(COSTS[6]),
        name="merge_tiles",
    )(span, mlist, arrived, out)


def work_list(value, stage):
    entries = value.size
    ids = jnp.arange(entries, dtype=jnp.int32)
    key = (stage + 1) * entries - ids
    rank = jnp.sum((key[None, :] < key[:, None]).astype(jnp.int32), axis=1).astype(jnp.int32)
    ordered = jnp.sum(jnp.where(rank[None, :] == ids[:, None], value[None, :], 0), axis=1)
    return jnp.pad(ordered.astype(jnp.int32), (0, UNROLL)), rank


def window_starts(cuts, sizes):
    sent = jnp.array([sum(sizes[:w]) for w in range(len(sizes) + 1)], jnp.int32)
    later = sent[:, None] - sent[None, :]
    reach = jnp.where(later >= 0, cuts[..., None, :] + later, jnp.int32(1 << 30))
    return jnp.min(reach, axis=-1).astype(jnp.int32)


def hop_plan(blocks):
    hops = blocks // CHUNK
    stages = [(t, t + 1) for t in range(0, hops, 2)]
    return tuple(range(0, blocks + 1, CHUNK)), tuple(stages)


def paired_shards(yields, partners):
    snaps_local, columns = yields.shape
    blocks = columns // BLOCK
    snap_count, bond_count = lax.axis_size("snap"), lax.axis_size("bond")
    total_snaps = snaps_local * snap_count
    q, d = lax.axis_index("snap"), lax.axis_index("bond")
    odd = lax.rem(d, 2).astype(jnp.int32)[None]
    slots = partners.shape[1] // snap_count
    bounds, takes = hop_plan(blocks)
    hops = len(bounds) - 1
    far_blocks = REACH - 1 - blocks
    stages = len(takes) + 1
    windows = (3 * WINDOW, WINDOW + 8) + (WINDOW, WINDOW + 12, WINDOW + 8)
    cfg = {
        "entries": blocks * slots,
        "spans": tuple((bounds[hop[0]], bounds[hop[-1] + 1]) for hop in takes),
        "slots": slots,
        "blocks": blocks,
        "bounds": bounds,
        "windows": windows,
        "stages": stages,
        "cut_m": 0,
        "cut_o": stages + 1,
        "win_o": 2 * (stages + 1),
        "win_m": 3 * (stages + 1),
        "inverse": 1.0 / (total_snaps - 1),
    }

    def other_core(value):
        return lax.ppermute(value, "snap", [(s, s ^ 1) for s in range(snap_count)])

    def across(value):
        return lax.ppermute(value, "snap", [(s, s ^ 2) for s in range(snap_count)])

    def other_chip(value):
        return across(value.astype(jnp.float16)).astype(F32)

    far, near = [None] * hops, [None] * hops

    def send_far(t, value):
        far[t] = lax.ppermute(value, "bond", [(s, s - 2) for s in range(2, bond_count)])

    def send_near(t, value):
        near[t] = lax.ppermute(value, "bond", [(s, s ^ 1) for s in range(bond_count)])

    second, mark = feed(cfg, (("own", 1),), odd, yields, yields)
    send_far(1, second)
    first, mark = feed(cfg, (("own", 0),), odd, yields, yields, mark)
    send_far(0, first)

    def step(t, *marks):
        plan = (("pick", t),)
        if t < hops - 2:
            plan += (("own", t + 2),)
        made = feed(cfg, plan, odd, yields, far[t], *marks)
        send_near(t, made[0])
        if len(plan) == 2:
            send_far(t + 2, made[1])
        return made[-1]

    sums = column_sums(yields, mark)
    sums = sums + other_core(sums)
    totals = sums + across(sums)
    bond_means = totals / total_snaps
    xa = centered_transposed(yields, bond_means)
    xb = other_core(xa)

    rel = partners - d * blocks
    live = partners >= 0
    halo_block = jnp.where(rel < 2 * blocks, rel - blocks, rel - 2 * blocks)
    ends = jnp.array([end for _, end in cfg["spans"][:-1]], jnp.int32)
    taken = jnp.sum((halo_block[..., None] >= ends).astype(jnp.int32), axis=-1)
    stage = jnp.where(live, jnp.where(rel < blocks, 0, taken + 1), stages)
    groups = stage.reshape(blocks, snap_count, slots)
    marks = jnp.arange(stages + 1, dtype=jnp.int32)
    cuts = jnp.sum((groups[..., None] < marks).astype(jnp.int32), axis=(0, 2))
    starts = window_starts(cuts, windows)
    left = jnp.max(cuts[:, -1] - starts[:, -1])

    def row_of(table, owner):
        return lax.dynamic_index_in_dim(table, owner, 0, keepdims=False)

    def listed(owner):
        def cut(a):
            return lax.dynamic_slice_in_dim(a, owner * slots, slots, axis=1)

        rows = lax.broadcasted_iota(jnp.int32, (blocks, slots), 0)
        value = rows * 4096 + lax.broadcasted_iota(jnp.int32, (blocks, slots), 1) * 256
        value, when = value + cut(jnp.where(live, rel, 0)), cut(stage)
        ordered, rank = work_list(value.reshape(-1), when.reshape(-1))
        return value, when, ordered, rank.reshape(blocks, slots)

    mvalue, mstage, mlist, _ = listed(q)
    ovalue, ostage, _, orank = listed(q ^ 2)
    ovalue = ovalue + (2 * orank + 1) * (1 << 18)
    work, _ = work_list(
        jnp.concatenate([ovalue, mvalue], axis=1).reshape(-1),
        jnp.concatenate([ostage, mstage], axis=1).reshape(-1),
    )
    mcuts, mwin, owin = row_of(cuts, q), row_of(starts, q), row_of(starts, q ^ 2)
    info = jnp.concatenate([mcuts, row_of(cuts, q ^ 2), owin, mwin])
    vote = left.astype(jnp.int32)[None]

    def center(group, *marks):
        raw, spans = [], []
        for kind, came, limit in ((0, near, blocks), (1, far, far_blocks)):
            for t in takes[group]:
                if bounds[t] < limit:
                    raw.append(came[t])
                    spans.append((kind, bounds[t], bounds[t + 1] - bounds[t]))
        mine, mark = join((near_mean, far_mean), raw, tuple(spans), *marks)
        return (mine, other_core(mine)), mark

    mark = step(0, mark)
    mark = step(1, mark)
    block_means = bond_means.reshape(blocks, BLOCK)
    out, send, window, mark = own_stage(cfg, info, mlist, work, xa, xb, mark)
    mark = step(2, mark)
    block_means = held_means(block_means, mark)
    near_mean = from_behind(block_means, "bond", -1)
    far_mean = from_behind(block_means, "bond", -2)
    arrived = {0: other_chip(window)}
    fed, merged = 3, 0
    for group, hop in enumerate(takes):
        while fed < hops and fed <= hop[-1] + 1:
            mark = step(fed, mark, *[arrived[w] for w in SEEN.get(fed, ())])
            fed += 1
        last = group + 1 == len(takes)
        halves, mark = center(group, mark)
        if fed < hops and len(hop) == 2:
            mark = step(fed, mark, *[arrived[w] for w in SEEN.get(fed, ())])
            fed += 1
        elif last:
            mark = rest(mark)
        merges = tuple(w for w in sorted(arrived) if merged <= w < group)
        merged = max((*merges, merged - 1)) + 1
        out, send, mark, vote, window = halo_stage(
            cfg, group + 1, merges, info, mlist, work, vote, xa, xb, halves,
            [arrived[w] for w in merges], out, send, mark,
        )
        if window is not None:
            arrived[group + 1] = other_chip(window)
    for stride in range((bond_count - 1).bit_length()):
        pairs = [(s, s ^ (1 << stride)) for s in range(bond_count)]
        vote = jnp.maximum(vote, lax.ppermute(vote, "bond", pairs))
    for w in sorted(arrived):
        if w >= merged:
            out = merge(cfg, mwin[w : w + 2], mlist, arrived[w], out)

    trips = (vote[0] + WINDOW - 1) // WINDOW

    def more(state):
        return state[0] < trips

    def turn(state):
        trip, result = state
        at = jnp.minimum(owin[-1] + trip * WINDOW, send.shape[0] - WINDOW)
        got = other_chip(lax.dynamic_slice_in_dim(send, at, WINDOW, axis=0))
        lo = jnp.minimum(mwin[-1] + trip * WINDOW, mcuts[-1])
        hi = jnp.minimum(lo + WINDOW, mcuts[-1])
        return trip + 1, merge(cfg, jnp.stack([lo, hi]), mlist, got, result)

    _, out = lax.while_loop(more, turn, (jnp.int32(0), out))
    return (bond_means, out)


def shards(yields, partners):
    blocks = yields.shape[1] // BLOCK
    snap_count, bond_count = lax.axis_size("snap"), lax.axis_size("bond")
    two_hops = blocks < REACH - 1 <= 2 * blocks
    if (
        two_hops
        and snap_count == 4
        and bond_count & (bond_count - 1) == 0
        and blocks % (2 * CHUNK) == 0
        and blocks // CHUNK >= 4
        and blocks <= 64
        and partners.shape[1] <= 64
        and blocks % PARTS == 0
        and partners.shape[1] % snap_count == 0
        and yields.shape[0] % BLOCK == 0
    ):
        return paired_shards(yields, partners)
    return plain_shards(yields, partners)


def solution(mesh):
    return jax.shard_map(
        shards,
        mesh=mesh,
        in_specs=(P("snap", "bond"), P("bond", None)),
        out_specs=(P("bond"), P("snap", "bond", None, None)),
        check_vma=False,
    )
```
